32 devices in a mesh: ctx: 2 (over core), ep: 16 (over z, y, x).
Axes of the slice: x: 2, y: 2, z: 4, core: 2. Of those that a mesh axis runs over, the one named last changes fastest.
Arguments:
- queries: bfloat16 [4096, 2048], P(('ctx', 'ep')), may hold values from -40 to 40
- keys: bfloat16 [4096, 256], P(('ctx', 'ep')), may hold values from -40 to 40
- values: bfloat16 [4096, 256], P(('ctx', 'ep')), may hold values from -6 to 6
- prior_out: bfloat16 [4096, 2048], P(('ctx', 'ep')), may hold values from -6 to 6
- prior_lse: float32 [4096, 16], P(('ctx', 'ep')), may hold values from 4 to 8
- residual: bfloat16 [4096, 2048], P(('ctx', 'ep')), may hold values from -40 to 40
- out_proj: bfloat16 [2048, 2048], P(('ctx', 'ep')), may hold values from -0.25 to 0.25
- norm_gain: float32 [2048], replicated, may hold values from 0.5 to 1.5
- expert_in: bfloat16 [16, 2048, 1536], P('ep'), may hold values from -0.125 to 0.125
- expert_out: bfloat16 [16, 768, 2048], P('ep'), may hold values from -0.21875 to 0.21875
- expert_ids: int32 [4096, 8], P(('ctx', 'ep')), may hold values from 0 to 15, as said below
- route_weight: float32 [4096, 8], P(('ctx', 'ep')), may hold values from 0.05 to 0.6
Outputs:
- layer_out: bfloat16 [4096, 2048], P(('ctx', 'ep'))
- attended: bfloat16 [4096, 2048], P(('ctx', 'ep'))
The draws below stay inside these ranges and needn't reach their ends.
Inputs may be any that keep to these rules, and one draw needn't show every extreme that they name: `expert_ids`: each row names 8 different experts. In the rows of one device no expert is named more than 72 times, and one expert is named exactly 72 times in the rows of every device.
All inputs are finite; a program needn't handle non-finite values.
Results may differ from the reference program's by a relative error of at most 0.0061.
Values may be sent and summed in bfloat16 or wider, within the bound.
No kernel may reach another device: no remote copies, remote signals or barrier semaphores. Data moves between devices by JAX's collectives and lax.ppermute only.
A program may use at most 128 MiB of HBM per device.

```python
import math
import jax
import jax.numpy as jnp
from jax import lax

D = 2048
HEADS = 16
KVH = 2
HD = 128
FFW = 768
TOP = 8
TOK_DEV = 128
GROUP = 8
STEPS = 1
EXPERTS = 16
CAP = 72
TOKENS = 4096
N_CTX = 2
N_EP = 16


def base_keys(key):
    normal_keys = jax.random.normal(jax.random.fold_in(key, 11), (TOKENS, KVH * HD), jnp.float32)
    return jnp.clip(normal_keys, -6.0, 6.0)


def draw_keys(key, part):
    values_out = base_keys(key)
    return values_out.astype(jnp.bfloat16)


def draw_queries(key, part):
    normal_q = jax.random.normal(jax.random.fold_in(key, 12), (TOKENS, HEADS * HD), jnp.float32)
    values_out = 2.0 * jnp.clip(normal_q, -6.0, 6.0)
    return values_out.astype(jnp.bfloat16)


def draw_residual(key, part):
    normal_x = jnp.clip(jax.random.normal(jax.random.fold_in(key, 21), (TOKENS, D), jnp.float32), -6.0, 6.0)
    col_scale = jnp.exp(jax.random.uniform(jax.random.fold_in(key, 22), (D,), jnp.float32, math.log(0.3), math.log(3.0)))
    row_scale = jnp.exp(jax.random.uniform(jax.random.fold_in(key, 23), (TOKENS, 1), jnp.float32, math.log(0.5), math.log(2.0)))
    values_out = 0.5 * row_scale * col_scale * normal_x
    return jnp.clip(values_out, -40.0, 40.0).astype(jnp.bfloat16)


def draw_expert_ids(key, part):
    block_count = TOKENS // TOK_DEV
    others = EXPERTS - 1
    hot_expert = jax.random.randint(jax.random.fold_in(key, 31), (), 0, EXPERTS, jnp.int32)

    def permute_rows(sub_key):
        return jax.random.permutation(sub_key, TOK_DEV).astype(jnp.int32)

    def permute_labels(sub_key):
        return jax.random.permutation(sub_key, others).astype(jnp.int32)
    row_order = jax.vmap(permute_rows)(jax.random.split(jax.random.fold_in(key, 32), block_count))
    heavy_rows = jax.vmap(permute_rows)(jax.random.split(jax.random.fold_in(key, 33), block_count)) < CAP
    labels = jax.vmap(permute_labels)(jax.random.split(jax.random.fold_in(key, 34), block_count))
    pick_steps = jnp.arange(TOP, dtype=jnp.int32)
    offsets = (row_order[:, :, None] % others + pick_steps[None, None, :]) % others

    def label_of(label_row, offset_rows):
        return label_row[offset_rows]
    picked = jax.vmap(label_of)(labels, offsets)
    names = (hot_expert + 1 + picked) % EXPERTS
    names = jnp.where(jnp.logical_and(heavy_rows[:, :, None], pick_steps[None, None, :] == TOP - 1), hot_expert, names)
    rotate = jax.random.randint(jax.random.fold_in(key, 35), (block_count, TOK_DEV, 1), 0, TOP, jnp.int32)
    names = jnp.take_along_axis(names, (pick_steps[None, None, :] + rotate) % TOP, axis=2)
    return names.reshape(TOKENS, TOP).astype(jnp.int32)


def with_spikes(drawn, stream_key, source, target, parts, factor):
    def block_of(dim):
        return (jnp.arange(drawn.shape[dim]) // (drawn.shape[dim] // parts)).reshape((-1,) + (1,) * (drawn.ndim - 1 - dim))

    near = jax.random.permutation(stream_key, parts)[block_of(target)]
    far = (block_of(target) + parts // 2) % parts
    return jnp.where((block_of(source) == near) | (block_of(source) == far), factor * drawn, drawn)


def shard_levels(key, extent, cuts, low, high):
    def one(axis_at, blocks):
        steps = jax.random.uniform(jax.random.fold_in(jax.random.fold_in(key, 6), axis_at), (blocks,), jnp.float32, low / len(cuts), high / len(cuts))
        return jnp.repeat(jnp.exp(steps), extent[axis_at] // blocks).reshape((-1,) + (1,) * (len(extent) - axis_at - 1))

    gain = one(*cuts[0])
    for cut in cuts[1:]:
        gain = gain * one(*cut)
    return gain


def centred(own_key, extent, deviation, limit, cuts=(), kind=jnp.bfloat16):
    values = deviation * jax.random.normal(own_key, extent, jnp.float32)
    if cuts:
        values = values * shard_levels(own_key, extent, cuts, -0.22, 0.18)
    return jnp.clip(values, -limit, limit).astype(kind)


def noise_with(stream_key, dims, scale, most, pieces, heavy, kind=jnp.bfloat16):
    values = scale * jax.random.normal(stream_key, dims, jnp.float32)
    if pieces:
        values = values * shard_levels(stream_key, dims, pieces, -0.22, 0.18)
    return jnp.clip(with_spikes(values, jax.random.fold_in(stream_key, 3), *heavy), -most, most).astype(kind)


def setup_inputs(seed: int = 0) -> dict:
    key_of = jax.random.split(jax.random.key(seed), 13)
    return {
        "queries": draw_queries(jax.random.fold_in(key_of[12], 71), 0),
        "keys": draw_keys(jax.random.fold_in(key_of[12], 71), 0),
        "values": centred(key_of[2], (TOKENS, KVH * HD), 1.0, 6.0, ((0, 32),)),
        "prior_out": centred(key_of[3], (TOKENS, HEADS * HD), 0.5, 6.0, ((0, 32),)),
        "prior_lse": jnp.clip(4.0 + 4.0 * jax.random.uniform(key_of[4], (TOKENS, HEADS), jnp.float32) ** shard_levels(key_of[4], (TOKENS, HEADS), ((0, 32),), -0.2, 0.2), 4.0, 8.0),
        "residual": draw_residual(jax.random.fold_in(key_of[12], 71), 0),
        "out_proj": noise_with(key_of[6], (HEADS * HD, D), (HEADS * HD) ** -0.5, 0.25, ((0, 32),), (0, 1, 32, 2.75)),
        "norm_gain": jnp.clip(1.0 + 0.1 * jax.random.normal(key_of[7], (D,), jnp.float32), 0.5, 1.5),
        "expert_in": centred(key_of[8], (EXPERTS, D, 2 * FFW), D ** -0.5, 0.125, ((0, 16),)),
        "expert_out": centred(key_of[9], (EXPERTS, FFW, D), FFW ** -0.5, 0.21875, ((0, 16),)),
        "expert_ids": draw_expert_ids(jax.random.fold_in(key_of[12], 71), 0),
        "route_weight": jnp.clip(jnp.exp(math.log(0.6) - 2.4849067 * jax.random.uniform(key_of[11], (TOKENS, TOP), jnp.float32) ** shard_levels(key_of[11], (TOKENS, TOP), ((0, 32),), -0.2, 0.2)), 0.05, 0.6),
    }


def attend_group(ctx_index, query_all, key_all, value_all, prior_all, lse_all):
    query_blk = query_all[ctx_index].reshape(N_EP, TOK_DEV, KVH, GROUP, HD).astype(jnp.float32)
    sources = [(ctx_index - stride) % N_CTX for stride in range(1, STEPS + 1)]
    key_win = jnp.concatenate([key_all[src_idx] for src_idx in sources], axis=1)
    key_win = key_win.reshape(N_EP, STEPS * TOK_DEV, KVH, HD).astype(jnp.float32)
    value_win = jnp.concatenate([value_all[src_idx] for src_idx in sources], axis=1)
    value_win = value_win.reshape(N_EP, STEPS * TOK_DEV, KVH, HD).astype(jnp.float32)
    scores = jnp.einsum('eighd,ejgd->eghij', query_blk, key_win) / math.sqrt(HD)
    query_local = jnp.arange(TOK_DEV, dtype=jnp.int32)[:, None]
    key_local = (jnp.arange(STEPS * TOK_DEV, dtype=jnp.int32) % TOK_DEV)[None, :]
    key_ctx = jnp.concatenate([jnp.zeros((TOK_DEV,), jnp.int32) + src_idx for src_idx in sources])[None, :]
    visible = (key_local < query_local) | (key_local == query_local) & (key_ctx <= ctx_index)
    scores = jnp.where(visible, scores, -jnp.inf)
    lse_prior = lse_all[ctx_index].reshape(N_EP, TOK_DEV, KVH, GROUP).transpose(0, 2, 3, 1)
    top_score = jnp.maximum(lse_prior, lax.optimization_barrier(jnp.max(scores, axis=-1)))
    weights = jnp.exp(scores - top_score[..., None])
    prior_weight = jnp.exp(lse_prior - top_score)
    totals = prior_weight + lax.optimization_barrier(jnp.sum(weights, axis=-1))
    weights_bf = lax.optimization_barrier(weights.astype(jnp.bfloat16)).astype(jnp.float32)
    gathered = jnp.einsum('eghij,ejgd->eighd', weights_bf, value_win)
    prior_part = prior_all[ctx_index].reshape(N_EP, TOK_DEV, KVH, GROUP, HD).astype(jnp.float32)
    prior_part = prior_part * prior_weight.transpose(0, 3, 1, 2)[..., None]
    result = (prior_part + gathered) / totals.transpose(0, 3, 1, 2)[..., None]
    return result.astype(jnp.bfloat16).reshape(N_EP, TOK_DEV, HEADS * HD)

def reference(queries, keys, values, prior_out, prior_lse, residual, out_proj, norm_gain, expert_in, expert_out, expert_ids, route_weight):

    def shaped(array):
        return array.reshape(N_CTX, N_EP, TOK_DEV, array.shape[-1])
    query_all = shaped(queries)
    key_all = shaped(keys)
    value_all = shaped(values)
    prior_all = shaped(prior_out)
    lse_all = shaped(prior_lse)

    def one_group(ctx_index):
        return attend_group(ctx_index, query_all, key_all, value_all, prior_all, lse_all)
    attended = lax.map(one_group, jnp.arange(N_CTX, dtype=jnp.int32)).reshape(TOKENS, HEADS * HD)
    mixed_state = (residual.astype(jnp.float32) + jnp.dot(attended, out_proj, preferred_element_type=jnp.float32)).astype(jnp.bfloat16)
    state_f = lax.optimization_barrier(mixed_state).astype(jnp.float32)
    normed = (state_f * lax.rsqrt(lax.optimization_barrier(jnp.mean(state_f * state_f, axis=-1, keepdims=True)) + 1e-06) * norm_gain).astype(jnp.bfloat16)
    flat_ids = expert_ids.reshape(-1)
    flat_weight = route_weight.reshape(-1)
    most_rows = N_CTX * N_EP * CAP

    def one_expert(summed, expert):
        chosen = flat_ids == expert
        picked = jnp.nonzero(chosen, size=most_rows, fill_value=0)[0].astype(jnp.int32)
        filled = jnp.arange(most_rows, dtype=jnp.int32) < jnp.sum(chosen.astype(jnp.int32))
        token_idx = picked // TOP
        inputs = normed[token_idx].astype(jnp.float32)
        gate_up = jnp.dot(inputs, expert_in[expert].astype(jnp.float32), preferred_element_type=jnp.float32)
        activated = (jax.nn.silu(gate_up[:, :FFW]) * gate_up[:, FFW:]).astype(jnp.bfloat16)
        replies = jnp.dot(activated.astype(jnp.float32), expert_out[expert].astype(jnp.float32), preferred_element_type=jnp.float32).astype(jnp.bfloat16)
        scaling = jnp.where(filled, flat_weight[picked], jnp.zeros((), flat_weight.dtype))
        summed = summed.at[token_idx].add(scaling[:, None] * replies.astype(jnp.float32))
        return (summed, None)
    summed, unused = lax.scan(one_expert, jnp.zeros((TOKENS, D), jnp.float32), jnp.arange(EXPERTS, dtype=jnp.int32))
    layer_out = (state_f + summed).astype(jnp.bfloat16)
    return (layer_out, attended)
```

```python
import math

import jax
import jax.numpy as jnp
from jax import lax
from jax.sharding import PartitionSpec as P

HEADS = 16
KVH = 2
HD = 128
GROUP = 8


def passed_along(shard, axis, by):
    devices = lax.axis_size(axis)
    return lax.ppermute(shard, axis, [(i, (i + by) % devices) for i in range(devices)])


def swapped(shard, axis, mask):
    devices = lax.axis_size(axis)
    return lax.ppermute(shard, axis, [(i, i ^ mask) for i in range(devices)])


def relative_columns(array, index, count):
    rows, columns = array.shape
    width = columns // count
    bit = 1
    while bit < count:
        pairs = array.reshape(rows, count // (2 * bit), 2, bit * width)
        turned = pairs[:, :, ::-1].reshape(rows, columns)
        array = jnp.where((index & bit) != 0, turned, array)
        bit *= 2
    return array


def attention(queries, keys, values, prior_out, prior_lse):
    local_rows = queries.shape[0]
    ctx_count = lax.axis_size("ctx")
    ctx_here = lax.axis_index("ctx")
    reach_steps = min(2, ctx_count - 1)
    kv_pair = jnp.stack([keys, values])
    arrived = []
    current = kv_pair
    for stride in range(reach_steps):
        current = passed_along(current, "ctx", 1)
        arrived.append(current)
    window = jnp.concatenate(arrived, axis=1)
    width_kv = window.shape[1]
    key_win = window[0].reshape(width_kv, KVH, HD)
    value_win = window[1].reshape(width_kv, KVH, HD)
    query_blk = queries.reshape(local_rows, KVH, GROUP, HD)
    scores = jnp.einsum(
        "ighd,jgd->ghij", query_blk, key_win, preferred_element_type=jnp.float32
    ) / math.sqrt(HD)
    positions = jnp.arange(width_kv, dtype=jnp.int32)
    key_local = positions % local_rows
    key_ctx = (ctx_here - (positions // local_rows + 1)) % ctx_count
    query_local = jnp.arange(local_rows, dtype=jnp.int32)[:, None]
    visible = (key_local[None, :] < query_local) | (key_local[None, :] == query_local) & (
        key_ctx[None, :] <= ctx_here
    )
    scores = jnp.where(visible, scores, -jnp.inf)
    lse_prior = prior_lse.reshape(local_rows, KVH, GROUP).transpose(1, 2, 0)
    top_score = jnp.maximum(lse_prior, jnp.max(scores, axis=-1))
    weights = jnp.exp(scores - top_score[..., None])
    prior_weight = jnp.exp(lse_prior - top_score)
    totals = prior_weight + jnp.sum(weights, axis=-1)
    gathered = jnp.einsum(
        "ghij,jgd->ighd",
        weights.astype(jnp.bfloat16),
        value_win,
        preferred_element_type=jnp.float32,
    )
    prior_part = (
        prior_out.reshape(local_rows, KVH, GROUP, HD).astype(jnp.float32)
        * prior_weight.transpose(2, 0, 1)[..., None]
    )
    attended = ((prior_part + gathered) / totals.transpose(2, 0, 1)[..., None]).astype(jnp.bfloat16)
    return attended.reshape(local_rows, HEADS * HD)


def plane_blocks(shard):
    ep_count = lax.axis_size("ep")
    columns = [(0, shard)]
    bit = ep_count // 2
    while bit >= 4:
        columns = columns + [(mask | bit, swapped(block, "ep", bit)) for mask, block in columns]
        bit //= 2
    planes = []
    half = shard.shape[0] // 2
    for mask, block in columns:
        beside = swapped(block, "ep", 1)
        behind = swapped(block, "ep", 2)
        across = [swapped(beside[:half], "ep", 2), swapped(behind[half:], "ep", 1)]
        planes.append((mask, jnp.concatenate([block, beside, behind] + across, axis=0)))
    return planes


def projected_rows(attended, out_proj):
    ctx_count = lax.axis_size("ctx")
    if ctx_count != 2 or out_proj.shape[0] % 32:
        full = lax.all_gather(out_proj, ("ctx", "ep"), axis=0, tiled=True)
        return jnp.dot(attended, full, preferred_element_type=jnp.float32)
    ep_count = lax.axis_size("ep")
    ep_here = lax.axis_index("ep")
    first = lax.axis_index("ctx") == 0
    planes = plane_blocks(out_proj)
    middle = attended.shape[1] // 2
    left, right = attended[:, :middle], attended[:, middle:]
    kept = jnp.where(first, left, right)
    sibling = swapped(jnp.where(first, right, left), "ctx", 1)
    kept = relative_columns(kept, ep_here, ep_count)
    sibling = relative_columns(sibling, ep_here, ep_count)
    rows = out_proj.shape[0]
    own_sum = 0.0
    sibling_sum = 0.0
    for mask, weight in planes:
        span = slice(mask * rows, (mask + 4) * rows)
        sibling_sum += jnp.dot(sibling[:, span], weight, preferred_element_type=jnp.float32)
        own_sum += jnp.dot(kept[:, span], weight, preferred_element_type=jnp.float32)
    return own_sum + swapped(sibling_sum, "ctx", 1)


def routing(expert_ids, route_weight, capacity):
    local_rows = expert_ids.shape[0]
    ep_count = lax.axis_size("ep")
    ep_here = lax.axis_index("ep")
    hits = expert_ids[:, :, None] == jnp.arange(ep_count, dtype=jnp.int32)
    weight_of = jnp.sum(jnp.where(hits, route_weight[:, :, None], 0.0), axis=1).T
    chosen = jnp.any(hits, axis=1).T
    order = jnp.arange(local_rows, dtype=jnp.int32)
    earlier = (order[:, None] < order[None, :]).astype(jnp.bfloat16)
    slot = jnp.dot(chosen.astype(jnp.bfloat16), earlier, preferred_element_type=jnp.float32)
    slot = jnp.where(chosen, slot, -1.0)
    experts = jnp.arange(ep_count, dtype=jnp.int32)
    told = jnp.stack([slot, slot[experts ^ 1], weight_of], axis=1)
    heard = lax.all_to_all(told, "ep", split_axis=0, concat_axis=0, tiled=True)
    masks = 2 * jnp.arange(ep_count // 2, dtype=jnp.int32)
    same_side = heard[ep_here ^ masks]
    other_side = heard[ep_here ^ masks ^ 1]
    places = jnp.arange(capacity, dtype=jnp.int32).astype(jnp.float32)[None, :, None]
    pack = (same_side[:, 1][:, None, :] == places).astype(jnp.bfloat16)
    own_weight = same_side[:, 2]
    slot_weight = jnp.sum(
        jnp.where(other_side[:, 0][:, None, :] == places, other_side[:, 2][:, None, :], 0.0), axis=2
    )
    return pack, own_weight, slot_weight


def run_expert(rows, row_weight, weight_in, weight_out):
    hidden_units = weight_out.shape[0]
    gate_up = jnp.dot(rows, weight_in, preferred_element_type=jnp.float32)
    activated = jax.nn.silu(gate_up[:, :hidden_units]) * gate_up[:, hidden_units:]
    activated = (activated * row_weight[:, None]).astype(jnp.bfloat16)
    return jnp.dot(activated, weight_out, preferred_element_type=jnp.float32)


def experts_sum(normed, pack, own_weight, slot_weight, weight_in, weight_out):
    ep_count = lax.axis_size("ep")
    local_rows, width = normed.shape
    capacity = pack.shape[1]
    blocks = {0: normed}
    bit = ep_count // 2
    while bit >= 2:
        for mask in list(blocks):
            blocks[mask | bit] = swapped(blocks[mask], "ep", bit)
        bit //= 2
    partial = {}
    for mask in sorted(blocks):
        if mask & 2:
            continue
        pair = (mask, mask | 2)
        arrived = []
        for m in pair:
            packed = jnp.dot(pack[m // 2], blocks[m], preferred_element_type=jnp.float32)
            arrived.append(swapped(packed.astype(jnp.bfloat16), "ep", 1))
        rows = jnp.concatenate([blocks[m] for m in pair] + arrived, axis=0)
        row_weight = jnp.concatenate(
            [own_weight[m // 2] for m in pair] + [slot_weight[m // 2] for m in pair]
        )
        replies = run_expert(rows, row_weight, weight_in, weight_out)
        returned = swapped(replies[2 * local_rows :].astype(jnp.bfloat16), "ep", 1)
        for i, m in enumerate(pair):
            partial[m] = replies[i * local_rows : (i + 1) * local_rows] + lax.dot_general(
                pack[m // 2],
                returned[i * capacity : (i + 1) * capacity],
                (((0,), (0,)), ((), ())),
                preferred_element_type=jnp.float32,
            )
    bit = 2
    while bit < ep_count:
        for mask in sorted(partial):
            if mask & bit:
                continue
            partial[mask] = partial[mask] + swapped(
                partial.pop(mask | bit).astype(jnp.bfloat16), "ep", bit
            ).astype(jnp.float32)
        bit *= 2
    return partial[0]


def shards(
    queries,
    keys,
    values,
    prior_out,
    prior_lse,
    residual,
    out_proj,
    norm_gain,
    expert_in,
    expert_out,
    expert_ids,
    route_weight,
):
    local_rows = queries.shape[0]
    experts_all = lax.axis_size("ep") * expert_in.shape[0]
    top_count = expert_ids.shape[1]
    capacity = max(
        local_rows // 4, top_count * ((local_rows + experts_all - 2) // (experts_all - 1))
    )
    attended = attention(queries, keys, values, prior_out, prior_lse)
    pack, own_weight, slot_weight = routing(expert_ids, route_weight, capacity)
    projected = projected_rows(attended, out_proj)
    mixed_state = (residual.astype(jnp.float32) + projected).astype(jnp.bfloat16)
    state_f = lax.optimization_barrier(mixed_state).astype(jnp.float32)
    normed = (
        state_f * lax.rsqrt(jnp.mean(state_f * state_f, axis=-1, keepdims=True) + 1e-06) * norm_gain
    ).astype(jnp.bfloat16)
    combined = experts_sum(normed, pack, own_weight, slot_weight, expert_in[0], expert_out[0])
    layer_out = (state_f + combined).astype(jnp.bfloat16)
    return (layer_out, attended)


def solution(mesh):
    return jax.shard_map(
        shards,
        mesh=mesh,
        in_specs=(
            P(("ctx", "ep"), None),
            P(("ctx", "ep"), None),
            P(("ctx", "ep"), None),
            P(("ctx", "ep"), None),
            P(("ctx", "ep"), None),
            P(("ctx", "ep"), None),
            P(("ctx", "ep"), None),
            P(),
            P("ep", None, None),
            P("ep", None, None),
            P(("ctx", "ep"), None),
            P(("ctx", "ep"), None),
        ),
        out_specs=(P(("ctx", "ep"), None), P(("ctx", "ep"), None)),
        check_vma=False,
    )
```

```python
import functools
import math

import jax
import jax.numpy as jnp
from jax import lax
from jax.experimental import pallas as pl
from jax.experimental.pallas import tpu as pltpu
from jax.sharding import PartitionSpec as P

HEADS = 16
KVH = 2
HD = 128
GROUP = 8


def passed_along(shard, axis, by):
    devices = lax.axis_size(axis)
    return lax.ppermute(shard, axis, [(i, (i + by) % devices) for i in range(devices)])


def swapped(shard, axis, mask):
    devices = lax.axis_size(axis)
    return lax.ppermute(shard, axis, [(i, i ^ mask) for i in range(devices)])


def after(array, *others):
    return lax.optimization_barrier((array,) + others)[0]


WHOLE = pl.BlockSpec(memory_space=pltpu.VMEM)
ANYWHERE = pl.BlockSpec(memory_space=pl.ANY)
SCALARS = pl.BlockSpec(memory_space=pltpu.SMEM)
ROOM = pltpu.CompilerParams(vmem_limit_bytes=16 * 1024 * 1024)
LARGE = pltpu.CompilerParams(vmem_limit_bytes=30 * 1024 * 1024)
BRIEF = pl.CostEstimate(flops=0, bytes_accessed=0, transcendentals=0)


def local(kernel, out_shape, *operands, room=ROOM):
    return pl.pallas_call(
        kernel,
        out_shape=out_shape,
        in_specs=[WHOLE] * len(operands),
        out_specs=jax.tree.map(lambda _: WHOLE, out_shape),
        compiler_params=room,
        cost_estimate=BRIEF,
    )(*operands)


def attention_kernel(here, queries, keys, values, prior_out, prior_lse, mask, *outs, count):
    halves = HEADS // 2
    hidden = mask[...]
    scale = 1.0 / math.sqrt(HD)
    relative = len(outs) > 1
    turn = (here[1] & 1) != 0
    flip = here[1] // (count // halves) if relative else 0
    for side in range(2):
        group = here[0] ^ (1 - side) if relative else side
        shared = pl.ds(pl.multiple_of(group * HD, HD), HD)
        lse_rows = prior_lse[pl.ds(pl.multiple_of(group * halves, halves), halves), :]
        spans, weights, prior_rows, total_rows = [], [], [], []
        for i in range(halves):
            head = group * halves + (i ^ flip)
            span = pl.ds(pl.multiple_of(head * HD, HD), HD)
            scores = lax.dot_general(
                keys[:, shared],
                queries[:, span],
                (((1,), (1,)), ((), ())),
                preferred_element_type=jnp.float32,
            )
            scores = scores * scale + hidden
            lse = prior_lse[pl.ds(head, 1), :]
            top = jnp.maximum(lse, jnp.max(scores, axis=0, keepdims=True))
            part = jnp.exp(scores - top)
            prior_weight = jnp.exp(lse - top)
            inverse = 1.0 / (prior_weight + jnp.sum(part, axis=0, keepdims=True))
            spans.append(span)
            weights.append(part.astype(jnp.bfloat16))
            prior_rows.append(prior_weight * inverse)
            total_rows.append(inverse)
        rows = jnp.concatenate(prior_rows + total_rows, axis=0)
        fill = jnp.zeros((HD - rows.shape[0], rows.shape[1]), jnp.float32)
        rows = jnp.concatenate([rows, fill], axis=0).T
        for i in range(halves):
            gathered = lax.dot_general(
                weights[i],
                values[:, shared],
                (((0,), (0,)), ((), ())),
                preferred_element_type=jnp.float32,
            )
            prior_part = rows[:, i : i + 1] * prior_out[:, spans[i]].astype(jnp.float32)
            result = prior_part + rows[:, halves + i : halves + i + 1] * gathered
            outs[0][:, spans[i]] = result.astype(jnp.bfloat16)
            if relative:
                turned = pltpu.roll(result, HD // 2, 1)
                outs[1 + side][:, i * HD : (i + 1) * HD] = jnp.where(turn, turned, result).astype(
                    jnp.bfloat16
                )


def attention(queries, keys, values, prior_out, prior_lse, split):
    rows, width = queries.shape
    ctx_count = lax.axis_size("ctx")
    ctx_here = lax.axis_index("ctx")
    reach_steps = min(2, ctx_count - 1)
    windows = []
    for array in (keys, values):
        arrived = []
        for stride in range(reach_steps):
            array = passed_along(array, "ctx", 1)
            arrived.append(array)
        windows.append(arrived[0] if reach_steps == 1 else jnp.concatenate(arrived, axis=0))
    positions = jnp.arange(reach_steps * rows, dtype=jnp.int32)[:, None]
    key_local = positions % rows
    key_ctx = (ctx_here - (positions // rows + 1)) % ctx_count
    query_local = jnp.arange(rows, dtype=jnp.int32)[None, :]
    visible = (key_local < query_local) | (key_local == query_local) & (key_ctx <= ctx_here)
    mask = jnp.where(visible, 0.0, -jnp.inf).astype(jnp.float32)
    here = jnp.stack([ctx_here, lax.axis_index("ep")]).astype(jnp.int32)
    shapes = [jax.ShapeDtypeStruct((rows, width), jnp.bfloat16)]
    if split:
        shapes += [jax.ShapeDtypeStruct((rows, width // 2), jnp.bfloat16)] * 2
    return pl.pallas_call(
        functools.partial(attention_kernel, count=lax.axis_size("ep")),
        out_shape=shapes,
        in_specs=[SCALARS] + [WHOLE] * 6,
        out_specs=[WHOLE] * len(shapes),
        compiler_params=ROOM,
        cost_estimate=BRIEF,
    )(here, queries, *windows, prior_out, prior_lse.T, mask)


WEIGHT_STEPS = (
    (8, 8),
    (2, 2),
    (1, 1),
    (4, 4),
    (12, 4),
    (None, 4),
    (10, 2),
    (9, 1),
    (None, 8),
    (3, 2),
    (5, 1),
    (None, 1),
    (14, 2),
    (6, 2),
    (None, 2),
    (13, 1),
    (11, 1),
    (7, 2),
    (15, 1),
)


def weight_planes(shard, picks, token):
    blocks = {0: shard}
    masks = [0]
    for mask, bit in WEIGHT_STEPS:
        if mask is None:
            token = after(swapped(picks, "ep", bit), token)
            picks = jnp.concatenate([picks, token], axis=0)
            masks = masks + [m | bit for m in masks]
        else:
            token = after(swapped(blocks[mask ^ bit], "ep", bit), token)
            blocks[mask] = token
    return [(m, [blocks[m + i] for i in range(4)]) for m in range(0, 16, 4)], picks, masks


def product_kernel(*refs, spans):
    lhs, blocks = refs[:2], refs[2 : 2 + 4 * len(spans)]
    outs, weight, sems = refs[2 + 4 * len(spans) : -2], refs[-2], refs[-1]
    rows, width = blocks[0].shape
    copies = []
    for i, block in enumerate(blocks):
        place = weight.at[pl.ds(i * rows, rows), :]
        copies.append(pltpu.make_async_copy(block, place, sems.at[i]))
        copies[-1].start()
    tile = min(width, 512)
    for i, span in enumerate(spans):
        for copy in copies[4 * i : 4 * i + 4]:
            copy.wait()
        left = jnp.concatenate([side[:, span] for side in lhs], axis=0)
        half = left.shape[0] // 2
        for start in range(0, width, tile):
            columns = slice(start, start + tile)
            term = jnp.dot(
                left,
                weight[4 * i * rows : 4 * (i + 1) * rows, columns],
                preferred_element_type=jnp.float32,
            )
            for out, part in zip(outs, (term[:half], term[half:])):
                out[:, columns] = part if i == 0 else out[:, columns] + part


def product(lhs, planes, rows):
    spans = [slice(mask * rows, (mask + 4) * rows) for mask, _ in planes]
    blocks = [block for _, plane in planes for block in plane]
    width = blocks[0].shape[1]
    shape = jax.ShapeDtypeStruct((lhs[0].shape[0], width), jnp.float32)
    return pl.pallas_call(
        functools.partial(product_kernel, spans=spans),
        out_shape=[shape] * 2,
        in_specs=[WHOLE] * 2 + [ANYWHERE] * len(blocks),
        out_specs=[WHOLE] * 2,
        scratch_shapes=[
            pltpu.VMEM((len(blocks) * rows, width), jnp.bfloat16),
            pltpu.SemaphoreType.DMA((len(blocks),)),
        ],
        compiler_params=ROOM,
        cost_estimate=BRIEF,
    )(*lhs, *blocks)


def norm_kernel(own, heard, residual, gain, pack, state, left, right, packed):
    mixed = (residual[...].astype(jnp.float32) + (own[...] + heard[...])).astype(jnp.bfloat16)
    state[...] = mixed
    mixed = mixed.astype(jnp.float32)
    scale = lax.rsqrt(jnp.mean(mixed * mixed, axis=1, keepdims=True) + 1e-06)
    rows = (mixed * scale * gain[...]).astype(jnp.bfloat16)
    middle = left.shape[1]
    left[...] = rows[:, :middle]
    right[...] = rows[:, middle:]
    packed[...] = jnp.dot(pack[0], rows, preferred_element_type=jnp.float32).astype(jnp.bfloat16)


def norm(own, heard, residual, gain, pack):
    rows, width = residual.shape
    half = jax.ShapeDtypeStruct((rows, width // 2), jnp.bfloat16)
    packed = jax.ShapeDtypeStruct((pack.shape[1], width), jnp.bfloat16)
    return local(
        norm_kernel,
        [jax.ShapeDtypeStruct(residual.shape, jnp.bfloat16), half, half, packed],
        own,
        heard,
        residual,
        gain.reshape(1, -1),
        pack,
    )


def routing_kernel(here, picks, pack, row_weight, *, masks):
    blocks, capacity, rows = pack.shape
    count, twice, _ = picks.shape
    ids, weights = picks[:, : twice // 2, :], picks[:, twice // 2 :, :]
    before = lax.broadcasted_iota(jnp.int32, (rows, rows), 0)
    behind = lax.broadcasted_iota(jnp.int32, (rows, rows), 1)
    earlier = jnp.where(before < behind, 1.0, 0.0).astype(jnp.bfloat16)
    places = lax.broadcasted_iota(jnp.int32, (capacity, rows), 0).astype(jnp.float32)

    def chosen(expert):
        hits = ids == expert.astype(jnp.float32)
        named = jnp.sum(jnp.where(hits, 1.0, 0.0), axis=1)
        slot = jnp.dot(named.astype(jnp.bfloat16), earlier, preferred_element_type=jnp.float32)
        return jnp.where(named > 0.0, slot, -1.0), jnp.sum(jnp.where(hits, weights, 0.0), axis=1)

    own_slot, own_weight = chosen(here[0])
    other_slot, _ = chosen(here[0] ^ 1)
    for m in range(blocks):
        same, other = masks.index(2 * m), masks.index(2 * m + 1)
        pack[m] = jnp.where(other_slot[same : same + 1] == places, 1.0, 0.0).astype(jnp.bfloat16)
        row = (m % 2) * rows
        row_weight[m // 2, row : row + rows, :] = jnp.sum(
            jnp.where(before == behind, own_weight[same : same + 1], 0.0), axis=1, keepdims=True
        )
        row = 2 * rows + (m % 2) * capacity
        row_weight[m // 2, row : row + capacity, :] = jnp.sum(
            jnp.where(
                own_slot[other : other + 1] == places, own_weight[other : other + 1], 0.0
            ),
            axis=1,
            keepdims=True,
        )


def own_picks(expert_ids, route_weight):
    return jnp.concatenate([expert_ids.T.astype(jnp.float32), route_weight.T], axis=0)[None]


def all_picks(picks):
    ep_count = lax.axis_size("ep")
    masks, bit = [0], 1
    while bit < ep_count:
        picks = jnp.concatenate([picks, swapped(picks, "ep", bit)], axis=0)
        masks = masks + [mask | bit for mask in masks]
        bit *= 2
    return picks, masks


def routing(picks, masks, capacity):
    count, _, rows = picks.shape
    return pl.pallas_call(
        functools.partial(routing_kernel, masks=masks),
        out_shape=[
            jax.ShapeDtypeStruct((count // 2, capacity, rows), jnp.bfloat16),
            jax.ShapeDtypeStruct((count // 4, 2 * rows + 2 * capacity, 1), jnp.float32),
        ],
        in_specs=[SCALARS, WHOLE],
        out_specs=[WHOLE] * 2,
        compiler_params=ROOM,
        cost_estimate=BRIEF,
    )(lax.axis_index("ep").astype(jnp.int32).reshape(1), picks)


def pack_kernel(index, pack, left, right, out):
    chosen = pack[index]
    middle = left.shape[1]
    for start, half in ((0, left), (middle, right)):
        rows = jnp.dot(chosen, half[...], preferred_element_type=jnp.float32)
        out[:, start : start + middle] = rows.astype(jnp.bfloat16)


def expert_kernel(*refs):
    near_left, near_right, far_left, far_right, near_packed, far_packed = refs[:6]
    row_weight, weight_in, weight_out, whole, near_out, far_out = refs[6:]
    near = jnp.concatenate([near_left[...], near_right[...]], axis=1)
    far = jnp.concatenate([far_left[...], far_right[...]], axis=1)
    packed = jnp.concatenate(
        [near_packed[...].astype(jnp.float32), far_packed[...].astype(jnp.float32)], axis=0
    ).astype(jnp.bfloat16)
    rows = jnp.concatenate([near, far, packed], axis=0)
    hidden_units, width = weight_out.shape
    tile = 256
    activated = []
    for start in range(0, hidden_units, tile):
        gate = jnp.dot(
            rows, weight_in[:, start : start + tile], preferred_element_type=jnp.float32
        )
        start += hidden_units
        up = jnp.dot(rows, weight_in[:, start : start + tile], preferred_element_type=jnp.float32)
        scaled = gate / (1.0 + jnp.exp(-gate)) * up * row_weight[...]
        activated.append(scaled.astype(jnp.bfloat16))
    activated = jnp.concatenate(activated, axis=1)
    count, capacity = whole.shape[0], near_out.shape[0]
    for start in range(0, width, tile):
        columns = slice(start, start + tile)
        reply = jnp.dot(activated, weight_out[:, columns], preferred_element_type=jnp.float32)
        whole[:, columns] = reply[:count]
        near_out[:, columns] = reply[count : count + capacity].astype(jnp.bfloat16)
        far_out[:, columns] = reply[count + capacity :].astype(jnp.bfloat16)


def unpack_kernel(index, far, pack, whole, returned, *outs):
    rows = pack.shape[2]
    total = lax.dot_general(
        pack[index],
        returned[...],
        (((0,), (0,)), ((), ())),
        preferred_element_type=jnp.float32,
    )
    total = total + whole[rows * far : rows * (far + 1), :]
    middle = outs[0].shape[1]
    for i, out in enumerate(outs):
        out[...] = total[:, i * middle : (i + 1) * middle].astype(out.dtype)


def final_kernel(state, *refs):
    parts, out = refs[:-1], refs[-1]
    middle = parts[0].shape[1]
    for i in range(2):
        columns = slice(i * middle, (i + 1) * middle)
        total = parts[i][...].astype(jnp.float32)
        for part in parts[2 + i :: 2]:
            total = total + part[...].astype(jnp.float32)
        out[:, columns] = (state[:, columns].astype(jnp.float32) + total).astype(jnp.bfloat16)


STEPS = (
    ("block", 2, 0),
    ("packed", 0),
    ("block", 2, 1),
    ("pack", 2),
    ("block", 4, 0),
    ("block", 8, 0),
    ("block", 4, 1),
    ("pack", 4),
    ("block", 8, 1),
    ("pack", 8),
    ("packed", 2),
    ("block", 6, 0),
    ("block", 12, 0),
    ("block", 10, 0),
    ("block", 6, 1),
    ("block", 12, 1),
    ("pack", 12),
    ("block", 14, 0),
    ("block", 10, 1),
    ("pack", 10),
    ("packed", 4),
    ("packed", 8),
    ("block", 14, 1),
    ("pack", 14),
    ("pack", 6),
    ("packed", 12),
    ("packed", 10),
    ("reply", 0),
    ("packed", 14),
)


def plain_steps(count):
    steps = []
    for mask in sorted(range(2, count, 2), key=lambda m: (m.bit_count(), m & 2, m)):
        steps += [("block", mask, 0), ("block", mask, 1), ("pack", mask)]
    return steps


def experts_sum(state, halves, packed, pack, row_weight, weight_in, weight_out):
    ep_count = lax.axis_size("ep")
    rows, width = state.shape
    capacity = pack.shape[1]
    half = (rows, width // 2)
    packed_shape = jax.ShapeDtypeStruct((capacity, width), jnp.bfloat16)
    blocks, arrived = {0: halves}, {0: swapped(packed, "ep", 1)}
    replies, returned = {}, {}
    token = packed

    def receive(mask, side):
        nonlocal token
        bit = mask & -mask
        token = after(swapped(blocks[mask ^ bit][side], "ep", bit), token)
        blocks.setdefault(mask, [None, None])[side] = token

    def send_packed(mask):
        nonlocal token
        token = local(
            functools.partial(pack_kernel, mask // 2),
            packed_shape,
            pack,
            blocks[mask][0],
            after(blocks[mask][1], token),
        )
        arrived[mask] = swapped(token, "ep", 1)

    def reply_to(mask):
        nonlocal token
        whole = jax.ShapeDtypeStruct((2 * rows, width), jnp.float32)
        replies[mask] = local(
            expert_kernel,
            [whole, packed_shape, packed_shape],
            after(blocks[mask][0], token),
            blocks[mask][1],
            *blocks[mask | 2],
            arrived[mask],
            arrived[mask | 2],
            row_weight[mask // 4],
            weight_in,
            weight_out,
            room=LARGE,
        )
        token = replies[mask][1]

    steps = STEPS if ep_count == 16 else plain_steps(ep_count)
    for kind, mask, *side in steps:
        if kind == "block":
            receive(mask, *side)
        elif kind == "pack":
            send_packed(mask)
        elif kind == "reply":
            reply_to(mask)
        else:
            token = arrived[mask] = after(arrived[mask], token)
    far = sorted(mask for mask in blocks if mask and not mask & 2)
    backward = [far[-1], far[-2]] + far[:-2][::-1] + [0]
    received = {mask: ([], []) for mask in backward}
    sums = {}

    def send_replies(mask):
        nonlocal token
        if mask not in replies:
            reply_to(mask)
        for far_side in (1, 0):
            token = after(replies[mask][1 + far_side], token)
            returned[mask | 2 * far_side] = swapped(token, "ep", 1)

    def unpack(mask):
        nonlocal token
        far_side = mask // 2 % 2
        kind = jnp.bfloat16 if far_side else jnp.float32
        outs = local(
            functools.partial(unpack_kernel, mask // 2, far_side),
            [jax.ShapeDtypeStruct(half, kind)] * 2,
            pack,
            replies[mask & ~2][0],
            after(returned[mask], token),
        )
        token = outs[0]
        if far_side:
            for side, out in enumerate(outs):
                received[mask & ~2][side].append(swapped(out, "ep", 2))
        else:
            sums[mask] = outs

    def pass_on(mask, side):
        nonlocal token
        total = sums[mask][side]
        for part in received[mask][side]:
            total = total + after(part, token).astype(jnp.float32)
        token = total.astype(jnp.bfloat16)
        bit = mask & -mask
        received[mask ^ bit][side].append(swapped(token, "ep", bit))

    for mask in backward[:2]:
        send_replies(mask)
    unpack(backward[0] | 2)
    for mask in backward[2:]:
        send_replies(mask)
    for k, mask in enumerate(backward):
        if k:
            unpack(mask | 2)
            pass_on(backward[k - 1], 0)
        if mask:
            unpack(mask)
        if k:
            pass_on(backward[k - 1], 1)
    unpack(0)
    parts = [part for pair in zip(*received[0]) for part in pair]
    shape = jax.ShapeDtypeStruct(state.shape, jnp.bfloat16)
    return local(final_kernel, shape, state, *sums[0], *parts)


def shards(
    queries,
    keys,
    values,
    prior_out,
    prior_lse,
    residual,
    out_proj,
    norm_gain,
    expert_in,
    expert_out,
    expert_ids,
    route_weight,
):
    local_rows = queries.shape[0]
    experts_all = lax.axis_size("ep") * expert_in.shape[0]
    top_count = expert_ids.shape[1]
    capacity = max(
        local_rows // 4, top_count * ((local_rows + experts_all - 2) // (experts_all - 1))
    )
    ep_count = lax.axis_size("ep")
    split = (
        lax.axis_size("ctx") == 2
        and out_proj.shape[0] * ep_count == HEADS // 2 * HD
        and 2 * out_proj.shape[0] == HD
    )
    picks = own_picks(expert_ids, route_weight)
    results = attention(queries, keys, values, prior_out, prior_lse, split)
    attended = results[0]
    if split:
        rows = out_proj.shape[0]
        given, kept = results[1:]
        sibling = swapped(given, "ctx", 1)
        planes, picks, masks = weight_planes(out_proj, picks, given)
        given_sum, own_sum = product([sibling, kept], planes, rows)
        heard_sum = swapped(given_sum, "ctx", 1)
    else:
        picks, masks = all_picks(picks)
        full = lax.all_gather(out_proj, ("ctx", "ep"), axis=0, tiled=True)
        own_sum = jnp.dot(attended, full, preferred_element_type=jnp.float32)
        heard_sum = jnp.zeros_like(own_sum)
    pack, row_weight = routing(picks, masks, capacity)
    state, left, right, packed = norm(own_sum, heard_sum, residual, norm_gain, pack)
    layer_out = experts_sum(
        state, [left, right], packed, pack, row_weight, expert_in[0], expert_out[0]
    )
    return (layer_out, attended)


def solution(mesh):
    return jax.shard_map(
        shards,
        mesh=mesh,
        in_specs=(
            P(("ctx", "ep"), None),
            P(("ctx", "ep"), None),
            P(("ctx", "ep"), None),
            P(("ctx", "ep"), None),
            P(("ctx", "ep"), None),
            P(("ctx", "ep"), None),
            P(("ctx", "ep"), None),
            P(),
            P("ep", None, None),
            P("ep", None, None),
            P(("ctx", "ep"), None),
            P(("ctx", "ep"), None),
        ),
        out_specs=(P(("ctx", "ep"), None), P(("ctx", "ep"), None)),
        check_vma=False,
    )
```

```python
import functools
import math

import jax
import jax.numpy as jnp
from jax import lax
from jax.experimental import pallas as pl
from jax.experimental.pallas import tpu as pltpu
from jax.sharding import PartitionSpec as P

HEADS = 16
KVH = 2
HD = 128
GROUP = 8


def passed_along(shard, axis, by):
    devices = lax.axis_size(axis)
    return lax.ppermute(shard, axis, [(i, (i + by) % devices) for i in range(devices)])


def swapped(shard, axis, mask):
    devices = lax.axis_size(axis)
    return lax.ppermute(shard, axis, [(i, i ^ mask) for i in range(devices)])


def after(array, *others):
    return lax.optimization_barrier((array,) + others)[0]


WHOLE = pl.BlockSpec(memory_space=pltpu.VMEM)
ANYWHERE = pl.BlockSpec(memory_space=pl.ANY)
SCALARS = pl.BlockSpec(memory_space=pltpu.SMEM)
ROOM = pltpu.CompilerParams(vmem_limit_bytes=16 * 1024 * 1024)
LARGE = pltpu.CompilerParams(vmem_limit_bytes=30 * 1024 * 1024)
BRIEF = pl.CostEstimate(flops=0, bytes_accessed=0, transcendentals=0)


def local(kernel, out_shape, *operands, room=ROOM):
    return pl.pallas_call(
        kernel,
        out_shape=out_shape,
        in_specs=[WHOLE] * len(operands),
        out_specs=jax.tree.map(lambda _: WHOLE, out_shape),
        compiler_params=room,
        cost_estimate=BRIEF,
    )(*operands)


def attention_kernel(here, queries, keys, values, prior_out, prior_lse, mask, *outs, count):
    halves = HEADS // 2
    hidden = mask[...]
    scale = 1.0 / math.sqrt(HD)
    relative = len(outs) > 1
    turn = (here[1] & 1) != 0
    flip = here[1] // (count // halves) if relative else 0
    for side in range(2):
        group = here[0] ^ (1 - side) if relative else side
        shared = pl.ds(pl.multiple_of(group * HD, HD), HD)
        lse_rows = prior_lse[pl.ds(pl.multiple_of(group * halves, halves), halves), :]
        spans, weights, prior_rows, total_rows = [], [], [], []
        for i in range(halves):
            head = group * halves + (i ^ flip)
            span = pl.ds(pl.multiple_of(head * HD, HD), HD)
            scores = lax.dot_general(
                keys[:, shared],
                queries[:, span],
                (((1,), (1,)), ((), ())),
                preferred_element_type=jnp.float32,
            )
            scores = scores * scale + hidden
            lse = prior_lse[pl.ds(head, 1), :]
            top = jnp.maximum(lse, jnp.max(scores, axis=0, keepdims=True))
            part = jnp.exp(scores - top)
            prior_weight = jnp.exp(lse - top)
            inverse = 1.0 / (prior_weight + jnp.sum(part, axis=0, keepdims=True))
            spans.append(span)
            weights.append(part.astype(jnp.bfloat16))
            prior_rows.append(prior_weight * inverse)
            total_rows.append(inverse)
        rows = jnp.concatenate(prior_rows + total_rows, axis=0)
        fill = jnp.zeros((HD - rows.shape[0], rows.shape[1]), jnp.float32)
        rows = jnp.concatenate([rows, fill], axis=0).T
        for i in range(halves):
            gathered = lax.dot_general(
                weights[i],
                values[:, shared],
                (((0,), (0,)), ((), ())),
                preferred_element_type=jnp.float32,
            )
            prior_part = rows[:, i : i + 1] * prior_out[:, spans[i]].astype(jnp.float32)
            result = prior_part + rows[:, halves + i : halves + i + 1] * gathered
            outs[0][:, spans[i]] = result.astype(jnp.bfloat16)
            if relative:
                turned = pltpu.roll(result, HD // 2, 1)
                outs[1 + side][:, i * HD : (i + 1) * HD] = jnp.where(turn, turned, result).astype(
                    jnp.bfloat16
                )


def attention(queries, keys, values, prior_out, prior_lse, split):
    rows, width = queries.shape
    ctx_count = lax.axis_size("ctx")
    ctx_here = lax.axis_index("ctx")
    reach_steps = min(2, ctx_count - 1)
    windows = []
    for array in (keys, values):
        arrived = []
        for stride in range(reach_steps):
            array = passed_along(array, "ctx", 1)
            arrived.append(array)
        windows.append(arrived[0] if reach_steps == 1 else jnp.concatenate(arrived, axis=0))
    positions = jnp.arange(reach_steps * rows, dtype=jnp.int32)[:, None]
    key_local = positions % rows
    key_ctx = (ctx_here - (positions // rows + 1)) % ctx_count
    query_local = jnp.arange(rows, dtype=jnp.int32)[None, :]
    visible = (key_local < query_local) | (key_local == query_local) & (key_ctx <= ctx_here)
    mask = jnp.where(visible, 0.0, -jnp.inf).astype(jnp.float32)
    here = jnp.stack([ctx_here, lax.axis_index("ep")]).astype(jnp.int32)
    shapes = [jax.ShapeDtypeStruct((rows, width), jnp.bfloat16)]
    if split:
        shapes += [jax.ShapeDtypeStruct((rows, width // 2), jnp.bfloat16)] * 2
    return pl.pallas_call(
        functools.partial(attention_kernel, count=lax.axis_size("ep")),
        out_shape=shapes,
        in_specs=[SCALARS] + [WHOLE] * 6,
        out_specs=[WHOLE] * len(shapes),
        compiler_params=ROOM,
        cost_estimate=BRIEF,
    )(here, queries, *windows, prior_out, prior_lse.T, mask)


WEIGHT_STEPS = (
    (8, 8),
    (2, 2),
    (1, 1),
    (4, 4),
    (9, 1),
    (12, 4),
    (10, 2),
    (5, 1),
    (3, 2),
    (None, 4),
    (14, 2),
    (13, 1),
    (None, 8),
    (6, 2),
    (15, 1),
    (11, 1),
    (7, 2),
)


def doubled(picks, masks, bit):
    picks = jnp.concatenate([picks, swapped(picks, "ep", bit)], axis=0)
    return picks, masks + [mask | bit for mask in masks]


def weight_planes(shard, picks, masks, token):
    blocks = {0: shard}
    for mask, bit in WEIGHT_STEPS:
        if mask is None:
            picks, masks = doubled(picks, masks, bit)
            token = after(picks, token)
            picks = token
        else:
            source = blocks[mask ^ bit]
            if mask == 6:
                source = after(source, blocks[12])
            token = after(swapped(source, "ep", bit), token)
            blocks[mask] = token
    return [(m, [blocks[m + i] for i in range(4)]) for m in range(0, 16, 4)], picks, masks


def product_kernel(*refs, spans):
    lhs, blocks = refs[:2], refs[2 : 2 + 4 * len(spans)]
    outs, weight, sems = refs[2 + 4 * len(spans) : -2], refs[-2], refs[-1]
    rows, width = blocks[0].shape
    copies = []
    for i, block in enumerate(blocks):
        place = weight.at[pl.ds(i * rows, rows), :]
        copies.append(pltpu.make_async_copy(block, place, sems.at[i]))
        copies[-1].start()
    tile = min(width, 512)
    for i, span in enumerate(spans):
        for copy in copies[4 * i : 4 * i + 4]:
            copy.wait()
        left = jnp.concatenate([side[:, span] for side in lhs], axis=0)
        half = left.shape[0] // 2
        for start in range(0, width, tile):
            columns = slice(start, start + tile)
            term = jnp.dot(
                left,
                weight[4 * i * rows : 4 * (i + 1) * rows, columns],
                preferred_element_type=jnp.float32,
            )
            for out, part in zip(outs, (term[:half], term[half:])):
                out[:, columns] = part if i == 0 else out[:, columns] + part


def product(lhs, planes, rows):
    spans = [slice(mask * rows, (mask + 4) * rows) for mask, _ in planes]
    blocks = [block for _, plane in planes for block in plane]
    width = blocks[0].shape[1]
    shape = jax.ShapeDtypeStruct((lhs[0].shape[0], width), jnp.float32)
    return pl.pallas_call(
        functools.partial(product_kernel, spans=spans),
        out_shape=[shape] * 2,
        in_specs=[WHOLE] * 2 + [ANYWHERE] * len(blocks),
        out_specs=[WHOLE] * 2,
        scratch_shapes=[
            pltpu.VMEM((len(blocks) * rows, width), jnp.bfloat16),
            pltpu.SemaphoreType.DMA((len(blocks),)),
        ],
        compiler_params=ROOM,
        cost_estimate=BRIEF,
    )(*lhs, *blocks)


def norm_kernel(own, heard, residual, gain, state, left, right):
    mixed = (residual[...].astype(jnp.float32) + (own[...] + heard[...])).astype(jnp.bfloat16)
    state[...] = mixed
    mixed = mixed.astype(jnp.float32)
    scale = lax.rsqrt(jnp.mean(mixed * mixed, axis=1, keepdims=True) + 1e-06)
    rows = (mixed * scale * gain[...]).astype(jnp.bfloat16)
    middle = left.shape[1]
    left[...] = rows[:, :middle]
    right[...] = rows[:, middle:]


def norm(own, heard, residual, gain):
    rows, width = residual.shape
    half = jax.ShapeDtypeStruct((rows, width // 2), jnp.bfloat16)
    return local(
        norm_kernel,
        [jax.ShapeDtypeStruct(residual.shape, jnp.bfloat16), half, half],
        own,
        heard,
        residual,
        gain.reshape(1, -1),
    )


def routing_kernel(here, picks, pack, row_weight, *, masks):
    blocks, capacity, rows = pack.shape
    count, twice, _ = picks.shape
    ids, weights = picks[:, : twice // 2, :], picks[:, twice // 2 :, :]
    before = lax.broadcasted_iota(jnp.int32, (rows, rows), 0)
    behind = lax.broadcasted_iota(jnp.int32, (rows, rows), 1)
    earlier = jnp.where(before < behind, 1.0, 0.0).astype(jnp.bfloat16)
    places = lax.broadcasted_iota(jnp.int32, (capacity, rows), 0).astype(jnp.float32)

    def chosen(expert):
        hits = ids == expert.astype(jnp.float32)
        named = jnp.sum(jnp.where(hits, 1.0, 0.0), axis=1)
        slot = jnp.dot(named.astype(jnp.bfloat16), earlier, preferred_element_type=jnp.float32)
        return jnp.where(named > 0.0, slot, -1.0), jnp.sum(jnp.where(hits, weights, 0.0), axis=1)

    own_slot, own_weight = chosen(here[0])
    other_slot, _ = chosen(here[0] ^ 1)
    for m in range(blocks):
        same, other = masks.index(2 * m), masks.index(2 * m + 1)
        pack[m] = jnp.where(other_slot[same : same + 1] == places, 1.0, 0.0).astype(jnp.bfloat16)
        row = (m % 2) * rows
        row_weight[m // 2, row : row + rows, :] = jnp.sum(
            jnp.where(before == behind, own_weight[same : same + 1], 0.0), axis=1, keepdims=True
        )
        row = 2 * rows + (m % 2) * capacity
        row_weight[m // 2, row : row + capacity, :] = jnp.sum(
            jnp.where(
                own_slot[other : other + 1] == places, own_weight[other : other + 1], 0.0
            ),
            axis=1,
            keepdims=True,
        )


def own_picks(expert_ids, route_weight):
    return jnp.concatenate([expert_ids.T.astype(jnp.float32), route_weight.T], axis=0)[None]


def all_picks(picks, masks, bits):
    for bit in bits:
        picks, masks = doubled(picks, masks, bit)
    return picks, masks


def routing(picks, masks, capacity):
    count, _, rows = picks.shape
    return pl.pallas_call(
        functools.partial(routing_kernel, masks=masks),
        out_shape=[
            jax.ShapeDtypeStruct((count // 2, capacity, rows), jnp.bfloat16),
            jax.ShapeDtypeStruct((count // 4, 2 * rows + 2 * capacity, 1), jnp.float32),
        ],
        in_specs=[SCALARS, WHOLE],
        out_specs=[WHOLE] * 2,
        compiler_params=ROOM,
        cost_estimate=BRIEF,
    )(lax.axis_index("ep").astype(jnp.int32).reshape(1), picks)


def pack_kernel(index, pack, left, right, out):
    chosen = pack[index]
    middle = left.shape[1]
    for start, half in ((0, left), (middle, right)):
        rows = jnp.dot(chosen, half[...], preferred_element_type=jnp.float32)
        out[:, start : start + middle] = rows.astype(jnp.bfloat16)


def expert_kernel(*refs):
    near_left, near_right, far_left, far_right, near_packed, far_packed = refs[:6]
    row_weight, weight_in, weight_out, whole, near_out, far_out = refs[6:]
    near = jnp.concatenate([near_left[...], near_right[...]], axis=1)
    far = jnp.concatenate([far_left[...], far_right[...]], axis=1)
    packed = jnp.concatenate(
        [near_packed[...].astype(jnp.float32), far_packed[...].astype(jnp.float32)], axis=0
    ).astype(jnp.bfloat16)
    rows = jnp.concatenate([near, far, packed], axis=0)
    hidden_units, width = weight_out.shape
    tile = 256
    activated = []
    for start in range(0, hidden_units, tile):
        gate = jnp.dot(
            rows, weight_in[:, start : start + tile], preferred_element_type=jnp.float32
        )
        start += hidden_units
        up = jnp.dot(rows, weight_in[:, start : start + tile], preferred_element_type=jnp.float32)
        scaled = gate / (1.0 + jnp.exp(-gate)) * up * row_weight[...]
        activated.append(scaled.astype(jnp.bfloat16))
    activated = jnp.concatenate(activated, axis=1)
    count, capacity = whole.shape[0], near_out.shape[0]
    for start in range(0, width, tile):
        columns = slice(start, start + tile)
        reply = jnp.dot(activated, weight_out[:, columns], preferred_element_type=jnp.float32)
        whole[:, columns] = reply[:count]
        near_out[:, columns] = reply[count : count + capacity].astype(jnp.bfloat16)
        far_out[:, columns] = reply[count + capacity :].astype(jnp.bfloat16)


def unpack_kernel(index, far, pack, whole, returned, *outs):
    rows = pack.shape[2]
    total = lax.dot_general(
        pack[index],
        returned[...],
        (((0,), (0,)), ((), ())),
        preferred_element_type=jnp.float32,
    )
    total = total + whole[rows * far : rows * (far + 1), :]
    middle = outs[0].shape[1]
    for i, out in enumerate(outs):
        out[...] = total[:, i * middle : (i + 1) * middle].astype(out.dtype)


def final_kernel(state, *refs):
    parts, out = refs[:-1], refs[-1]
    middle = parts[0].shape[1]
    for i in range(2):
        columns = slice(i * middle, (i + 1) * middle)
        total = parts[i][...].astype(jnp.float32)
        for part in parts[2 + i :: 2]:
            total = total + part[...].astype(jnp.float32)
        out[:, columns] = (state[:, columns].astype(jnp.float32) + total).astype(jnp.bfloat16)


STEPS = (
    ("block", 2, 0),
    ("pack", 0),
    ("block", 2, 1),
    ("pack", 2),
    ("block", 4, 0),
    ("block", 8, 0),
    ("block", 4, 1),
    ("pack", 4),
    ("block", 8, 1),
    ("pack", 8),
    ("packed", 0),
    ("packed", 2),
    ("block", 6, 0),
    ("block", 12, 0),
    ("block", 10, 0),
    ("block", 6, 1),
    ("block", 12, 1),
    ("pack", 12),
    ("block", 14, 0),
    ("block", 10, 1),
    ("pack", 10),
    ("packed", 4),
    ("packed", 8),
    ("block", 14, 1),
    ("pack", 14),
    ("pack", 6),
    ("packed", 12),
    ("packed", 10),
    ("reply", 0),
    ("packed", 14),
    ("reply", 12),
    ("packed", 6),
)


def plain_steps(count):
    steps = [("pack", 0)]
    for mask in sorted(range(2, count, 2), key=lambda m: (m.bit_count(), m & 2, m)):
        steps += [("block", mask, 0), ("block", mask, 1), ("pack", mask)]
    return steps


def experts_sum(state, halves, pack, row_weight, weight_in, weight_out):
    ep_count = lax.axis_size("ep")
    rows, width = state.shape
    capacity = pack.shape[1]
    half = (rows, width // 2)
    packed_shape = jax.ShapeDtypeStruct((capacity, width), jnp.bfloat16)
    blocks, arrived = {0: halves}, {}
    replies, returned = {}, {}
    token = state

    def receive(mask, side):
        nonlocal token
        bit = mask & -mask
        source = blocks[mask ^ bit][side]
        if mask == 2:
            source = after(source, pack)
        token = after(swapped(source, "ep", bit), token)
        blocks.setdefault(mask, [None, None])[side] = token

    def send_packed(mask):
        nonlocal token
        token = local(
            functools.partial(pack_kernel, mask // 2),
            packed_shape,
            pack,
            blocks[mask][0],
            after(blocks[mask][1], token),
        )
        arrived[mask] = swapped(token, "ep", 1)

    def reply_to(mask):
        nonlocal token
        whole = jax.ShapeDtypeStruct((2 * rows, width), jnp.float32)
        replies[mask] = local(
            expert_kernel,
            [whole, packed_shape, packed_shape],
            after(blocks[mask][0], token),
            blocks[mask][1],
            *blocks[mask | 2],
            arrived[mask],
            arrived[mask | 2],
            row_weight[mask // 4],
            weight_in,
            weight_out,
            room=LARGE,
        )
        token = replies[mask][1]

    steps = STEPS if ep_count == 16 else plain_steps(ep_count)
    for kind, mask, *side in steps:
        if kind == "block":
            receive(mask, *side)
        elif kind == "pack":
            send_packed(mask)
        elif kind == "reply":
            reply_to(mask)
        else:
            token = arrived[mask] = after(arrived[mask], token)
    far = sorted(mask for mask in blocks if mask and not mask & 2)
    backward = [far[-1], far[-2]] + far[:-2][::-1] + [0]
    received = {mask: ([], []) for mask in backward}
    sums = {}

    def send_reply(mask):
        nonlocal token
        group, far_side = mask & ~2, mask // 2 % 2
        if group not in replies:
            reply_to(group)
        token = after(replies[group][1 + far_side], token)
        returned[mask] = swapped(token, "ep", 1)

    def unpack(mask):
        nonlocal token
        far_side = mask // 2 % 2
        kind = jnp.bfloat16 if far_side else jnp.float32
        outs = local(
            functools.partial(unpack_kernel, mask // 2, far_side),
            [jax.ShapeDtypeStruct(half, kind)] * 2,
            pack,
            replies[mask & ~2][0],
            after(returned[mask], token),
        )
        token = outs[0]
        if far_side:
            for side, out in enumerate(outs):
                received[mask & ~2][side].append(swapped(out, "ep", 2))
        else:
            sums[mask] = outs

    def pass_on(mask, side):
        nonlocal token
        total = sums[mask][side]
        for part in received[mask][side]:
            total = total + after(part, token).astype(jnp.float32)
        token = total.astype(jnp.bfloat16)
        bit = mask & -mask
        received[mask ^ bit][side].append(swapped(token, "ep", bit))

    for mask in backward[:2]:
        send_reply(mask | 2)
        send_reply(mask)
    unpack(backward[0] | 2)
    for mask in backward[2:-1]:
        send_reply(mask | 2)
        send_reply(mask)
    unpack(backward[0])
    for k, mask in enumerate(backward[1:-1]):
        if k == 0:
            unpack(mask | 2)
        pass_on(backward[k], 0)
        if k == 1:
            send_reply(2)
        pass_on(backward[k], 1)
        if k == 0:
            unpack(mask)
            unpack(backward[2] | 2)
        else:
            if k > 1:
                unpack(mask | 2)
            unpack(mask)
    send_reply(0)
    pass_on(backward[-2], 0)
    pass_on(backward[-2], 1)
    near, far = received[0]
    token = near[0] = after(near[0], token)
    unpack(2)
    token = far[0] = after(far[0], token)
    token = near[1] = after(near[1], token)
    unpack(0)
    parts = [part for pair in zip(*received[0]) for part in pair]
    shape = jax.ShapeDtypeStruct(state.shape, jnp.bfloat16)
    return local(final_kernel, shape, state, *sums[0], *parts)


def shards(
    queries,
    keys,
    values,
    prior_out,
    prior_lse,
    residual,
    out_proj,
    norm_gain,
    expert_in,
    expert_out,
    expert_ids,
    route_weight,
):
    local_rows = queries.shape[0]
    experts_all = lax.axis_size("ep") * expert_in.shape[0]
    top_count = expert_ids.shape[1]
    capacity = max(
        local_rows // 4, top_count * ((local_rows + experts_all - 2) // (experts_all - 1))
    )
    ep_count = lax.axis_size("ep")
    split = (
        lax.axis_size("ctx") == 2
        and out_proj.shape[0] * ep_count == HEADS // 2 * HD
        and 2 * out_proj.shape[0] == HD
    )
    picks = own_picks(expert_ids, route_weight)
    masks = [0]
    results = attention(queries, keys, values, prior_out, prior_lse, split)
    attended = results[0]
    if split:
        rows = out_proj.shape[0]
        given, kept = results[1:]
        sibling = swapped(given, "ctx", 1)
        planes, picks, masks = weight_planes(out_proj, picks, masks, given)
        given_sum, own_sum = product([sibling, kept], planes, rows)
        picks, masks = doubled(picks, masks, 1)
        heard_sum = after(swapped(given_sum, "ctx", 1), picks)
        picks, masks = doubled(picks, masks, 2)
    else:
        picks, masks = all_picks(picks, masks, [1 << k for k in range(ep_count.bit_length() - 1)])
        full = lax.all_gather(out_proj, ("ctx", "ep"), axis=0, tiled=True)
        own_sum = jnp.dot(attended, full, preferred_element_type=jnp.float32)
        heard_sum = jnp.zeros_like(own_sum)
    pack, row_weight = routing(picks, masks, capacity)
    state, left, right = norm(own_sum, heard_sum, residual, norm_gain)
    layer_out = experts_sum(
        state, [left, right], pack, row_weight, expert_in[0], expert_out[0]
    )
    return (layer_out, attended)


def solution(mesh):
    return jax.shard_map(
        shards,
        mesh=mesh,
        in_specs=(
            P(("ctx", "ep"), None),
            P(("ctx", "ep"), None),
            P(("ctx", "ep"), None),
            P(("ctx", "ep"), None),
            P(("ctx", "ep"), None),
            P(("ctx", "ep"), None),
            P(("ctx", "ep"), None),
            P(),
            P("ep", None, None),
            P("ep", None, None),
            P(("ctx", "ep"), None),
            P(("ctx", "ep"), None),
        ),
        out_specs=(P(("ctx", "ep"), None), P(("ctx", "ep"), None)),
        check_vma=False,
    )
```

```python
import functools
import math

import jax
import jax.numpy as jnp
from jax import lax
from jax.experimental import pallas as pl
from jax.experimental.pallas import tpu as pltpu
from jax.sharding import PartitionSpec as P

HEADS = 16
KVH = 2
HD = 128
GROUP = 8


def passed_along(shard, axis, by):
    devices = lax.axis_size(axis)
    return lax.ppermute(shard, axis, [(i, (i + by) % devices) for i in range(devices)])


def swapped(shard, axis, mask):
    devices = lax.axis_size(axis)
    return lax.ppermute(shard, axis, [(i, i ^ mask) for i in range(devices)])


def after(array, *others):
    return lax.optimization_barrier((array,) + others)[0]


WHOLE = pl.BlockSpec(memory_space=pltpu.VMEM)
ANYWHERE = pl.BlockSpec(memory_space=pl.ANY)
SCALARS = pl.BlockSpec(memory_space=pltpu.SMEM)
ROOM = pltpu.CompilerParams(vmem_limit_bytes=16 * 1024 * 1024)
LARGE = pltpu.CompilerParams(vmem_limit_bytes=30 * 1024 * 1024)
BRIEF = pl.CostEstimate(flops=0, bytes_accessed=0, transcendentals=0)


def local(kernel, out_shape, *operands, room=ROOM):
    return pl.pallas_call(
        kernel,
        out_shape=out_shape,
        in_specs=[WHOLE] * len(operands),
        out_specs=jax.tree.map(lambda _: WHOLE, out_shape),
        compiler_params=room,
        cost_estimate=BRIEF,
    )(*operands)


def attention_kernel(here, queries, keys, values, prior_out, prior_lse, mask, *outs, count):
    halves = HEADS // 2
    hidden = mask[...]
    scale = 1.0 / math.sqrt(HD)
    relative = len(outs) > 1
    turn = (here[1] & 1) != 0
    flip = here[1] // (count // halves) if relative else 0
    for side in range(2):
        group = here[0] ^ (1 - side) if relative else side
        shared = pl.ds(pl.multiple_of(group * HD, HD), HD)
        lse_rows = prior_lse[pl.ds(pl.multiple_of(group * halves, halves), halves), :]
        spans, weights, prior_rows, total_rows = [], [], [], []
        for i in range(halves):
            head = group * halves + (i ^ flip)
            span = pl.ds(pl.multiple_of(head * HD, HD), HD)
            scores = lax.dot_general(
                keys[:, shared],
                queries[:, span],
                (((1,), (1,)), ((), ())),
                preferred_element_type=jnp.float32,
            )
            scores = scores * scale + hidden
            lse = prior_lse[pl.ds(head, 1), :]
            top = jnp.maximum(lse, jnp.max(scores, axis=0, keepdims=True))
            part = jnp.exp(scores - top)
            prior_weight = jnp.exp(lse - top)
            inverse = 1.0 / (prior_weight + jnp.sum(part, axis=0, keepdims=True))
            spans.append(span)
            weights.append(part.astype(jnp.bfloat16))
            prior_rows.append(prior_weight * inverse)
            total_rows.append(inverse)
        rows = jnp.concatenate(prior_rows + total_rows, axis=0)
        fill = jnp.zeros((HD - rows.shape[0], rows.shape[1]), jnp.float32)
        rows = jnp.concatenate([rows, fill], axis=0).T
        for i in range(halves):
            gathered = lax.dot_general(
                weights[i],
                values[:, shared],
                (((0,), (0,)), ((), ())),
                preferred_element_type=jnp.float32,
            )
            prior_part = rows[:, i : i + 1] * prior_out[:, spans[i]].astype(jnp.float32)
            result = prior_part + rows[:, halves + i : halves + i + 1] * gathered
            outs[0][:, spans[i]] = result.astype(jnp.bfloat16)
            if relative:
                turned = pltpu.roll(result, HD // 2, 1)
                outs[1 + side][:, i * HD : (i + 1) * HD] = jnp.where(turn, turned, result).astype(
                    jnp.bfloat16
                )


def attention(queries, keys, values, prior_out, prior_lse, split):
    rows, width = queries.shape
    ctx_count = lax.axis_size("ctx")
    ctx_here = lax.axis_index("ctx")
    reach_steps = min(2, ctx_count - 1)
    windows = []
    for array in (keys, values):
        arrived = []
        for stride in range(reach_steps):
            array = passed_along(array, "ctx", 1)
            arrived.append(array)
        windows.append(arrived[0] if reach_steps == 1 else jnp.concatenate(arrived, axis=0))
    positions = jnp.arange(reach_steps * rows, dtype=jnp.int32)[:, None]
    key_local = positions % rows
    key_ctx = (ctx_here - (positions // rows + 1)) % ctx_count
    query_local = jnp.arange(rows, dtype=jnp.int32)[None, :]
    visible = (key_local < query_local) | (key_local == query_local) & (key_ctx <= ctx_here)
    mask = jnp.where(visible, 0.0, -jnp.inf).astype(jnp.float32)
    here = jnp.stack([ctx_here, lax.axis_index("ep")]).astype(jnp.int32)
    shapes = [jax.ShapeDtypeStruct((rows, width), jnp.bfloat16)]
    if split:
        shapes += [jax.ShapeDtypeStruct((rows, width // 2), jnp.bfloat16)] * 2
    return pl.pallas_call(
        functools.partial(attention_kernel, count=lax.axis_size("ep")),
        out_shape=shapes,
        in_specs=[SCALARS] + [WHOLE] * 6,
        out_specs=[WHOLE] * len(shapes),
        compiler_params=ROOM,
        cost_estimate=BRIEF,
    )(here, queries, *windows, prior_out, prior_lse.T, mask)


WEIGHT_STEPS = (
    (8, 8),
    (2, 2),
    (1, 1),
    (4, 4),
    (9, 1),
    (12, 4),
    (10, 2),
    (5, 1),
    (3, 2),
    (None, 4),
    (13, 1),
    (14, 2),
    (None, 8),
    (11, 1),
    (6, 2),
    (15, 1),
    (7, 2),
)


def doubled(picks, masks, bit):
    picks = jnp.concatenate([picks, swapped(picks, "ep", bit)], axis=0)
    return picks, masks + [mask | bit for mask in masks]


def weight_planes(shard, picks, masks, token):
    blocks = {0: shard}
    for mask, bit in WEIGHT_STEPS:
        if mask is None:
            picks, masks = doubled(picks, masks, bit)
            token = after(picks, token)
            picks = token
        else:
            source = blocks[mask ^ bit]
            if mask == 6:
                source = after(source, blocks[12])
            token = after(swapped(source, "ep", bit), token)
            blocks[mask] = token
    return [(m, [blocks[m + i] for i in range(4)]) for m in range(0, 16, 4)], picks, masks


def product_kernel(*refs, spans):
    lhs, blocks = refs[:2], refs[2 : 2 + 4 * len(spans)]
    outs, weight, sems = refs[2 + 4 * len(spans) : -2], refs[-2], refs[-1]
    rows, width = blocks[0].shape
    copies = []
    for i, block in enumerate(blocks):
        place = weight.at[pl.ds(i * rows, rows), :]
        copies.append(pltpu.make_async_copy(block, place, sems.at[i]))
        copies[-1].start()
    tile = min(width, 512)
    for i, span in enumerate(spans):
        for copy in copies[4 * i : 4 * i + 4]:
            copy.wait()
        left = jnp.concatenate([side[:, span] for side in lhs], axis=0)
        half = left.shape[0] // 2
        for start in range(0, width, tile):
            columns = slice(start, start + tile)
            term = jnp.dot(
                left,
                weight[4 * i * rows : 4 * (i + 1) * rows, columns],
                preferred_element_type=jnp.float32,
            )
            for out, part in zip(outs, (term[:half], term[half:])):
                out[:, columns] = part if i == 0 else out[:, columns] + part


def product(lhs, planes, rows):
    spans = [slice(mask * rows, (mask + 4) * rows) for mask, _ in planes]
    blocks = [block for _, plane in planes for block in plane]
    width = blocks[0].shape[1]
    shape = jax.ShapeDtypeStruct((lhs[0].shape[0], width), jnp.float32)
    return pl.pallas_call(
        functools.partial(product_kernel, spans=spans),
        out_shape=[shape] * 2,
        in_specs=[WHOLE] * 2 + [ANYWHERE] * len(blocks),
        out_specs=[WHOLE] * 2,
        scratch_shapes=[
            pltpu.VMEM((len(blocks) * rows, width), jnp.bfloat16),
            pltpu.SemaphoreType.DMA((len(blocks),)),
        ],
        compiler_params=ROOM,
        cost_estimate=BRIEF,
    )(*lhs, *blocks)


def norm_kernel(own, heard, residual, gain, state, left, right):
    mixed = (residual[...].astype(jnp.float32) + (own[...] + heard[...])).astype(jnp.bfloat16)
    state[...] = mixed
    mixed = mixed.astype(jnp.float32)
    scale = lax.rsqrt(jnp.mean(mixed * mixed, axis=1, keepdims=True) + 1e-06)
    rows = (mixed * scale * gain[...]).astype(jnp.bfloat16)
    middle = left.shape[1]
    left[...] = rows[:, :middle]
    right[...] = rows[:, middle:]


def norm(own, heard, residual, gain):
    rows, width = residual.shape
    half = jax.ShapeDtypeStruct((rows, width // 2), jnp.bfloat16)
    return local(
        norm_kernel,
        [jax.ShapeDtypeStruct(residual.shape, jnp.bfloat16), half, half],
        own,
        heard,
        residual,
        gain.reshape(1, -1),
    )


def routing_kernel(here, picks, pack, row_weight, *, masks):
    blocks, capacity, rows = pack.shape
    count, twice, _ = picks.shape
    ids, weights = picks[:, : twice // 2, :], picks[:, twice // 2 :, :]
    before = lax.broadcasted_iota(jnp.int32, (rows, rows), 0)
    behind = lax.broadcasted_iota(jnp.int32, (rows, rows), 1)
    earlier = jnp.where(before < behind, 1.0, 0.0).astype(jnp.bfloat16)
    places = lax.broadcasted_iota(jnp.int32, (capacity, rows), 0).astype(jnp.float32)

    def chosen(expert):
        hits = ids == expert.astype(jnp.float32)
        named = jnp.sum(jnp.where(hits, 1.0, 0.0), axis=1)
        slot = jnp.dot(named.astype(jnp.bfloat16), earlier, preferred_element_type=jnp.float32)
        return jnp.where(named > 0.0, slot, -1.0), jnp.sum(jnp.where(hits, weights, 0.0), axis=1)

    own_slot, own_weight = chosen(here[0])
    other_slot, _ = chosen(here[0] ^ 1)
    for m in range(blocks):
        same, other = masks.index(2 * m), masks.index(2 * m + 1)
        pack[m] = jnp.where(other_slot[same : same + 1] == places, 1.0, 0.0).astype(jnp.bfloat16)
        row = (m % 2) * rows
        row_weight[m // 2, row : row + rows, :] = jnp.sum(
            jnp.where(before == behind, own_weight[same : same + 1], 0.0), axis=1, keepdims=True
        )
        row = 2 * rows + (m % 2) * capacity
        row_weight[m // 2, row : row + capacity, :] = jnp.sum(
            jnp.where(
                own_slot[other : other + 1] == places, own_weight[other : other + 1], 0.0
            ),
            axis=1,
            keepdims=True,
        )


def own_picks(expert_ids, route_weight):
    return jnp.concatenate([expert_ids.T.astype(jnp.float32), route_weight.T], axis=0)[None]


def all_picks(picks, masks, bits):
    for bit in bits:
        picks, masks = doubled(picks, masks, bit)
    return picks, masks


def routing(picks, masks, capacity):
    count, _, rows = picks.shape
    return pl.pallas_call(
        functools.partial(routing_kernel, masks=masks),
        out_shape=[
            jax.ShapeDtypeStruct((count // 2, capacity, rows), jnp.bfloat16),
            jax.ShapeDtypeStruct((count // 4, 2 * rows + 2 * capacity, 1), jnp.float32),
        ],
        in_specs=[SCALARS, WHOLE],
        out_specs=[WHOLE] * 2,
        compiler_params=ROOM,
        cost_estimate=BRIEF,
    )(lax.axis_index("ep").astype(jnp.int32).reshape(1), picks)


def pack_kernel(index, pack, left, right, out):
    chosen = pack[index]
    middle = left.shape[1]
    for start, half in ((0, left), (middle, right)):
        rows = jnp.dot(chosen, half[...], preferred_element_type=jnp.float32)
        out[:, start : start + middle] = rows.astype(jnp.bfloat16)


def expert_kernel(*refs):
    near_left, near_right, far_left, far_right, near_packed, far_packed = refs[:6]
    row_weight, weight_in, weight_out, whole, near_out, far_out = refs[6:]
    near = jnp.concatenate([near_left[...], near_right[...]], axis=1)
    far = jnp.concatenate([far_left[...], far_right[...]], axis=1)
    packed = jnp.concatenate(
        [near_packed[...].astype(jnp.float32), far_packed[...].astype(jnp.float32)], axis=0
    ).astype(jnp.bfloat16)
    rows = jnp.concatenate([near, far, packed], axis=0)
    hidden_units, width = weight_out.shape
    tile = 256
    activated = []
    for start in range(0, hidden_units, tile):
        gate = jnp.dot(
            rows, weight_in[:, start : start + tile], preferred_element_type=jnp.float32
        )
        start += hidden_units
        up = jnp.dot(rows, weight_in[:, start : start + tile], preferred_element_type=jnp.float32)
        scaled = gate / (1.0 + jnp.exp(-gate)) * up * row_weight[...]
        activated.append(scaled.astype(jnp.bfloat16))
    activated = jnp.concatenate(activated, axis=1)
    count, capacity = whole.shape[0], near_out.shape[0]
    for start in range(0, width, tile):
        columns = slice(start, start + tile)
        reply = jnp.dot(activated, weight_out[:, columns], preferred_element_type=jnp.float32)
        whole[:, columns] = reply[:count]
        near_out[:, columns] = reply[count : count + capacity].astype(jnp.bfloat16)
        far_out[:, columns] = reply[count + capacity :].astype(jnp.bfloat16)


def unpack_kernel(index, far, pack, whole, returned, *outs):
    rows = pack.shape[2]
    total = lax.dot_general(
        pack[index],
        returned[...],
        (((0,), (0,)), ((), ())),
        preferred_element_type=jnp.float32,
    )
    total = total + whole[rows * far : rows * (far + 1), :]
    middle = outs[0].shape[1]
    for i, out in enumerate(outs):
        out[...] = total[:, i * middle : (i + 1) * middle].astype(out.dtype)


def final_kernel(state, *refs):
    parts, out = refs[:-1], refs[-1]
    middle = parts[0].shape[1]
    for i in range(2):
        columns = slice(i * middle, (i + 1) * middle)
        total = parts[i][...].astype(jnp.float32)
        for part in parts[2 + i :: 2]:
            total = total + part[...].astype(jnp.float32)
        out[:, columns] = (state[:, columns].astype(jnp.float32) + total).astype(jnp.bfloat16)


STEPS = (
    ("block", 2, 0),
    ("pack", 0),
    ("block", 2, 1),
    ("pack", 2),
    ("block", 4, 0),
    ("block", 8, 0),
    ("block", 4, 1),
    ("pack", 4),
    ("block", 8, 1),
    ("pack", 8),
    ("packed", 0),
    ("packed", 2),
    ("block", 6, 0),
    ("block", 12, 0),
    ("block", 10, 0),
    ("block", 6, 1),
    ("block", 12, 1),
    ("pack", 12),
    ("block", 14, 0),
    ("block", 10, 1),
    ("pack", 10),
    ("packed", 4),
    ("packed", 8),
    ("block", 14, 1),
    ("pack", 14),
    ("pack", 6),
    ("packed", 12),
    ("packed", 10),
    ("reply", 0),
    ("packed", 14),
    ("reply", 12),
    ("packed", 6),
)


def plain_steps(count):
    steps = [("pack", 0)]
    for mask in sorted(range(2, count, 2), key=lambda m: (m.bit_count(), m & 2, m)):
        steps += [("block", mask, 0), ("block", mask, 1), ("pack", mask)]
    return steps


def experts_sum(state, halves, pack, row_weight, weight_in, weight_out):
    ep_count = lax.axis_size("ep")
    rows, width = state.shape
    capacity = pack.shape[1]
    half = (rows, width // 2)
    packed_shape = jax.ShapeDtypeStruct((capacity, width), jnp.bfloat16)
    blocks, arrived = {0: halves}, {}
    replies, returned = {}, {}
    token = state

    def receive(mask, side):
        nonlocal token
        bit = mask & -mask
        source = blocks[mask ^ bit][side]
        if mask == 2:
            source = after(source, pack)
        token = after(swapped(source, "ep", bit), token)
        blocks.setdefault(mask, [None, None])[side] = token

    def send_packed(mask):
        nonlocal token
        token = local(
            functools.partial(pack_kernel, mask // 2),
            packed_shape,
            pack,
            blocks[mask][0],
            after(blocks[mask][1], token),
        )
        arrived[mask] = swapped(token, "ep", 1)

    def reply_to(mask):
        nonlocal token
        whole = jax.ShapeDtypeStruct((2 * rows, width), jnp.float32)
        replies[mask] = local(
            expert_kernel,
            [whole, packed_shape, packed_shape],
            after(blocks[mask][0], token),
            blocks[mask][1],
            *blocks[mask | 2],
            arrived[mask],
            arrived[mask | 2],
            row_weight[mask // 4],
            weight_in,
            weight_out,
            room=LARGE,
        )
        token = replies[mask][1]

    steps = STEPS if ep_count == 16 else plain_steps(ep_count)
    for kind, mask, *side in steps:
        if kind == "block":
            receive(mask, *side)
        elif kind == "pack":
            send_packed(mask)
        elif kind == "reply":
            reply_to(mask)
        else:
            token = arrived[mask] = after(arrived[mask], token)
    far = sorted(mask for mask in blocks if mask and not mask & 2)
    backward = [far[-1], far[-2]] + far[:-2][::-1] + [0]
    received = {mask: ([], []) for mask in backward}
    sums = {}

    def send_reply(mask):
        nonlocal token
        group, far_side = mask & ~2, mask // 2 % 2
        if group not in replies:
            reply_to(group)
        token = after(replies[group][1 + far_side], token)
        returned[mask] = swapped(token, "ep", 1)

    def unpack(mask):
        nonlocal token
        far_side = mask // 2 % 2
        kind = jnp.bfloat16 if far_side else jnp.float32
        outs = local(
            functools.partial(unpack_kernel, mask // 2, far_side),
            [jax.ShapeDtypeStruct(half, kind)] * 2,
            pack,
            replies[mask & ~2][0],
            after(returned[mask], token),
        )
        token = outs[0]
        if far_side:
            for side, out in enumerate(outs):
                received[mask & ~2][side].append(swapped(out, "ep", 2))
        else:
            sums[mask] = outs

    def pass_on(mask, side):
        nonlocal token
        total = sums[mask][side]
        for part in received[mask][side]:
            total = total + after(part, token).astype(jnp.float32)
        token = total.astype(jnp.bfloat16)
        bit = mask & -mask
        received[mask ^ bit][side].append(swapped(token, "ep", bit))

    for mask in backward[:2]:
        send_reply(mask | 2)
        send_reply(mask)
    unpack(backward[0] | 2)
    for mask in backward[2:-1]:
        send_reply(mask | 2)
        send_reply(mask)
    unpack(backward[0])
    for k, mask in enumerate(backward[1:-1]):
        if k == 0:
            unpack(mask | 2)
        pass_on(backward[k], 0)
        if k == 1:
            send_reply(2)
        pass_on(backward[k], 1)
        if k == 0:
            unpack(mask)
            unpack(backward[2] | 2)
        else:
            if k > 1:
                unpack(mask | 2)
            unpack(mask)
    send_reply(0)
    pass_on(backward[-2], 0)
    pass_on(backward[-2], 1)
    near, far = received[0]
    token = near[0] = after(near[0], token)
    unpack(2)
    token = far[0] = after(far[0], token)
    token = near[1] = after(near[1], token)
    unpack(0)
    parts = [part for pair in zip(*received[0]) for part in pair]
    shape = jax.ShapeDtypeStruct(state.shape, jnp.bfloat16)
    return local(final_kernel, shape, state, *sums[0], *parts)


def shards(
    queries,
    keys,
    values,
    prior_out,
    prior_lse,
    residual,
    out_proj,
    norm_gain,
    expert_in,
    expert_out,
    expert_ids,
    route_weight,
):
    local_rows = queries.shape[0]
    experts_all = lax.axis_size("ep") * expert_in.shape[0]
    top_count = expert_ids.shape[1]
    capacity = max(
        local_rows // 4, top_count * ((local_rows + experts_all - 2) // (experts_all - 1))
    )
    ep_count = lax.axis_size("ep")
    split = (
        lax.axis_size("ctx") == 2
        and out_proj.shape[0] * ep_count == HEADS // 2 * HD
        and 2 * out_proj.shape[0] == HD
    )
    picks = own_picks(expert_ids, route_weight)
    masks = [0]
    results = attention(queries, keys, values, prior_out, prior_lse, split)
    attended = results[0]
    if split:
        rows = out_proj.shape[0]
        given, kept = results[1:]
        sibling = swapped(given, "ctx", 1)
        planes, picks, masks = weight_planes(out_proj, picks, masks, given)
        given_sum, own_sum = product([sibling, kept], planes, rows)
        heard_sum = swapped(given_sum, "ctx", 1)
        picks = jnp.concatenate([picks] + [swapped(picks, "ep", m) for m in (1, 2, 3)], axis=0)
        masks = [mask | m for m in range(4) for mask in masks]
    else:
        picks, masks = all_picks(picks, masks, [1 << k for k in range(ep_count.bit_length() - 1)])
        full = lax.all_gather(out_proj, ("ctx", "ep"), axis=0, tiled=True)
        own_sum = jnp.dot(attended, full, preferred_element_type=jnp.float32)
        heard_sum = jnp.zeros_like(own_sum)
    pack, row_weight = routing(picks, masks, capacity)
    state, left, right = norm(own_sum, heard_sum, residual, norm_gain)
    layer_out = experts_sum(
        state, [left, right], pack, row_weight, expert_in[0], expert_out[0]
    )
    return (layer_out, attended)


def solution(mesh):
    return jax.shard_map(
        shards,
        mesh=mesh,
        in_specs=(
            P(("ctx", "ep"), None),
            P(("ctx", "ep"), None),
            P(("ctx", "ep"), None),
            P(("ctx", "ep"), None),
            P(("ctx", "ep"), None),
            P(("ctx", "ep"), None),
            P(("ctx", "ep"), None),
            P(),
            P("ep", None, None),
            P("ep", None, None),
            P(("ctx", "ep"), None),
            P(("ctx", "ep"), None),
        ),
        out_specs=(P(("ctx", "ep"), None), P(("ctx", "ep"), None)),
        check_vma=False,
    )
```

```python
import functools
import math

import jax
import jax.numpy as jnp
from jax import lax
from jax.experimental import pallas as pl
from jax.experimental.pallas import tpu as pltpu
from jax.sharding import PartitionSpec as P

HEADS = 16
KVH = 2
HD = 128
GROUP = 8


def passed_along(shard, axis, by):
    devices = lax.axis_size(axis)
    return lax.ppermute(shard, axis, [(i, (i + by) % devices) for i in range(devices)])


def swapped(shard, axis, mask):
    devices = lax.axis_size(axis)
    return lax.ppermute(shard, axis, [(i, i ^ mask) for i in range(devices)])


def after(array, *others):
    return lax.optimization_barrier((array,) + others)[0]


WHOLE = pl.BlockSpec(memory_space=pltpu.VMEM)
ANYWHERE = pl.BlockSpec(memory_space=pl.ANY)
SCALARS = pl.BlockSpec(memory_space=pltpu.SMEM)
ROOM = pltpu.CompilerParams(vmem_limit_bytes=16 * 1024 * 1024)
LARGE = pltpu.CompilerParams(vmem_limit_bytes=30 * 1024 * 1024)
BRIEF = pl.CostEstimate(flops=0, bytes_accessed=0, transcendentals=0)


def local(kernel, out_shape, *operands, room=ROOM):
    return pl.pallas_call(
        kernel,
        out_shape=out_shape,
        in_specs=[WHOLE] * len(operands),
        out_specs=jax.tree.map(lambda _: WHOLE, out_shape),
        compiler_params=room,
        cost_estimate=BRIEF,
    )(*operands)


def attention_kernel(here, queries, keys, values, prior_out, prior_lse, mask, *outs, count):
    halves = HEADS // 2
    hidden = mask[...]
    scale = 1.0 / math.sqrt(HD)
    relative = len(outs) > 1
    turn = (here[1] & 1) != 0
    flip = here[1] // (count // halves) if relative else 0
    for side in range(2):
        group = here[0] ^ (1 - side) if relative else side
        shared = pl.ds(pl.multiple_of(group * HD, HD), HD)
        lse_rows = prior_lse[pl.ds(pl.multiple_of(group * halves, halves), halves), :]
        spans, weights, prior_rows, total_rows = [], [], [], []
        for i in range(halves):
            head = group * halves + (i ^ flip)
            span = pl.ds(pl.multiple_of(head * HD, HD), HD)
            scores = lax.dot_general(
                keys[:, shared],
                queries[:, span],
                (((1,), (1,)), ((), ())),
                preferred_element_type=jnp.float32,
            )
            scores = scores * scale + hidden
            lse = prior_lse[pl.ds(head, 1), :]
            top = jnp.maximum(lse, jnp.max(scores, axis=0, keepdims=True))
            part = jnp.exp(scores - top)
            prior_weight = jnp.exp(lse - top)
            inverse = 1.0 / (prior_weight + jnp.sum(part, axis=0, keepdims=True))
            spans.append(span)
            weights.append(part.astype(jnp.bfloat16))
            prior_rows.append(prior_weight * inverse)
            total_rows.append(inverse)
        rows = jnp.concatenate(prior_rows + total_rows, axis=0)
        fill = jnp.zeros((HD - rows.shape[0], rows.shape[1]), jnp.float32)
        rows = jnp.concatenate([rows, fill], axis=0).T
        for i in range(halves):
            gathered = lax.dot_general(
                weights[i],
                values[:, shared],
                (((0,), (0,)), ((), ())),
                preferred_element_type=jnp.float32,
            )
            prior_part = rows[:, i : i + 1] * prior_out[:, spans[i]].astype(jnp.float32)
            result = prior_part + rows[:, halves + i : halves + i + 1] * gathered
            outs[0][:, spans[i]] = result.astype(jnp.bfloat16)
            if relative:
                turned = pltpu.roll(result, HD // 2, 1)
                outs[1 + side][:, i * HD : (i + 1) * HD] = jnp.where(turn, turned, result).astype(
                    jnp.bfloat16
                )


def attention(queries, keys, values, prior_out, prior_lse, split):
    rows, width = queries.shape
    ctx_count = lax.axis_size("ctx")
    ctx_here = lax.axis_index("ctx")
    reach_steps = min(2, ctx_count - 1)
    windows = []
    for array in (keys, values):
        arrived = []
        for stride in range(reach_steps):
            array = passed_along(array, "ctx", 1)
            arrived.append(array)
        windows.append(arrived[0] if reach_steps == 1 else jnp.concatenate(arrived, axis=0))
    positions = jnp.arange(reach_steps * rows, dtype=jnp.int32)[:, None]
    key_local = positions % rows
    key_ctx = (ctx_here - (positions // rows + 1)) % ctx_count
    query_local = jnp.arange(rows, dtype=jnp.int32)[None, :]
    visible = (key_local < query_local) | (key_local == query_local) & (key_ctx <= ctx_here)
    mask = jnp.where(visible, 0.0, -jnp.inf).astype(jnp.float32)
    here = jnp.stack([ctx_here, lax.axis_index("ep")]).astype(jnp.int32)
    shapes = [jax.ShapeDtypeStruct((rows, width), jnp.bfloat16)]
    if split:
        shapes += [jax.ShapeDtypeStruct((rows, width // 2), jnp.bfloat16)] * 2
    return pl.pallas_call(
        functools.partial(attention_kernel, count=lax.axis_size("ep")),
        out_shape=shapes,
        in_specs=[SCALARS] + [WHOLE] * 6,
        out_specs=[WHOLE] * len(shapes),
        compiler_params=ROOM,
        cost_estimate=BRIEF,
    )(here, queries, *windows, prior_out, prior_lse.T, mask)


WEIGHT_STEPS = (
    (8, 8),
    (2, 2),
    (1, 1),
    (4, 4),
    (9, 1),
    (12, 4),
    (10, 2),
    (5, 1),
    (3, 2),
    (None, 4),
    (13, 1),
    (14, 2),
    (None, 8),
    (11, 1),
    (6, 2),
    (15, 1),
    (7, 2),
)


def doubled(picks, masks, bit):
    picks = jnp.concatenate([picks, swapped(picks, "ep", bit)], axis=0)
    return picks, masks + [mask | bit for mask in masks]


def weight_planes(shard, picks, masks, token):
    blocks = {0: shard}
    for mask, bit in WEIGHT_STEPS:
        if mask is None:
            picks, masks = doubled(picks, masks, bit)
            token = after(picks, token)
            picks = token
        else:
            source = blocks[mask ^ bit]
            if mask == 6:
                source = after(source, blocks[12])
            token = after(swapped(source, "ep", bit), token)
            blocks[mask] = token
    return [(m, [blocks[m + i] for i in range(4)]) for m in range(0, 16, 4)], picks, masks


def product_kernel(*refs, spans):
    lhs, blocks = refs[:2], refs[2 : 2 + 4 * len(spans)]
    outs, weight, sems = refs[2 + 4 * len(spans) : -2], refs[-2], refs[-1]
    rows, width = blocks[0].shape
    copies = []
    for i, block in enumerate(blocks):
        place = weight.at[pl.ds(i * rows, rows), :]
        copies.append(pltpu.make_async_copy(block, place, sems.at[i]))
        copies[-1].start()
    tile = min(width, 512)
    for i, span in enumerate(spans):
        for copy in copies[4 * i : 4 * i + 4]:
            copy.wait()
        left = jnp.concatenate([side[:, span] for side in lhs], axis=0)
        half = left.shape[0] // 2
        for start in range(0, width, tile):
            columns = slice(start, start + tile)
            term = jnp.dot(
                left,
                weight[4 * i * rows : 4 * (i + 1) * rows, columns],
                preferred_element_type=jnp.float32,
            )
            for out, part in zip(outs, (term[:half], term[half:])):
                out[:, columns] = part if i == 0 else out[:, columns] + part


def product(lhs, planes, rows):
    spans = [slice(mask * rows, (mask + 4) * rows) for mask, _ in planes]
    blocks = [block for _, plane in planes for block in plane]
    width = blocks[0].shape[1]
    shape = jax.ShapeDtypeStruct((lhs[0].shape[0], width), jnp.float32)
    return pl.pallas_call(
        functools.partial(product_kernel, spans=spans),
        out_shape=[shape] * 2,
        in_specs=[WHOLE] * 2 + [ANYWHERE] * len(blocks),
        out_specs=[WHOLE] * 2,
        scratch_shapes=[
            pltpu.VMEM((len(blocks) * rows, width), jnp.bfloat16),
            pltpu.SemaphoreType.DMA((len(blocks),)),
        ],
        compiler_params=ROOM,
        cost_estimate=BRIEF,
    )(*lhs, *blocks)


def norm_kernel(own, heard, residual, gain, state, left, right):
    mixed = (residual[...].astype(jnp.float32) + (own[...] + heard[...])).astype(jnp.bfloat16)
    state[...] = mixed
    mixed = mixed.astype(jnp.float32)
    scale = lax.rsqrt(jnp.mean(mixed * mixed, axis=1, keepdims=True) + 1e-06)
    rows = (mixed * scale * gain[...]).astype(jnp.bfloat16)
    middle = left.shape[1]
    left[...] = rows[:, :middle]
    right[...] = rows[:, middle:]


def norm(own, heard, residual, gain):
    rows, width = residual.shape
    half = jax.ShapeDtypeStruct((rows, width // 2), jnp.bfloat16)
    return local(
        norm_kernel,
        [jax.ShapeDtypeStruct(residual.shape, jnp.bfloat16), half, half],
        own,
        heard,
        residual,
        gain.reshape(1, -1),
    )


def routing_kernel(here, picks, pack, row_weight, *, masks):
    blocks, capacity, rows = pack.shape
    count, twice, _ = picks.shape
    ids, weights = picks[:, : twice // 2, :], picks[:, twice // 2 :, :]
    before = lax.broadcasted_iota(jnp.int32, (rows, rows), 0)
    behind = lax.broadcasted_iota(jnp.int32, (rows, rows), 1)
    earlier = jnp.where(before < behind, 1.0, 0.0).astype(jnp.bfloat16)
    places = lax.broadcasted_iota(jnp.int32, (capacity, rows), 0).astype(jnp.float32)

    def chosen(expert):
        hits = ids == expert.astype(jnp.float32)
        named = jnp.sum(jnp.where(hits, 1.0, 0.0), axis=1)
        slot = jnp.dot(named.astype(jnp.bfloat16), earlier, preferred_element_type=jnp.float32)
        return jnp.where(named > 0.0, slot, -1.0), jnp.sum(jnp.where(hits, weights, 0.0), axis=1)

    own_slot, own_weight = chosen(here[0])
    other_slot, _ = chosen(here[0] ^ 1)
    for m in range(blocks):
        same, other = masks.index(2 * m), masks.index(2 * m + 1)
        pack[m] = jnp.where(other_slot[same : same + 1] == places, 1.0, 0.0).astype(jnp.bfloat16)
        row = (m % 2) * rows
        row_weight[m // 2, row : row + rows, :] = jnp.sum(
            jnp.where(before == behind, own_weight[same : same + 1], 0.0), axis=1, keepdims=True
        )
        row = 2 * rows + (m % 2) * capacity
        row_weight[m // 2, row : row + capacity, :] = jnp.sum(
            jnp.where(
                own_slot[other : other + 1] == places, own_weight[other : other + 1], 0.0
            ),
            axis=1,
            keepdims=True,
        )


def own_picks(expert_ids, route_weight):
    return jnp.concatenate([expert_ids.T.astype(jnp.float32), route_weight.T], axis=0)[None]


def all_picks(picks, masks, bits):
    for bit in bits:
        picks, masks = doubled(picks, masks, bit)
    return picks, masks


def routing(picks, masks, capacity):
    count, _, rows = picks.shape
    return pl.pallas_call(
        functools.partial(routing_kernel, masks=masks),
        out_shape=[
            jax.ShapeDtypeStruct((count // 2, capacity, rows), jnp.bfloat16),
            jax.ShapeDtypeStruct((count // 4, 2 * rows + 2 * capacity, 1), jnp.float32),
        ],
        in_specs=[SCALARS, WHOLE],
        out_specs=[WHOLE] * 2,
        compiler_params=ROOM,
        cost_estimate=BRIEF,
    )(lax.axis_index("ep").astype(jnp.int32).reshape(1), picks)


def pack_kernel(index, pack, left, right, out):
    chosen = pack[index]
    middle = left.shape[1]
    for start, half in ((0, left), (middle, right)):
        rows = jnp.dot(chosen, half[...], preferred_element_type=jnp.float32)
        out[:, start : start + middle] = rows.astype(jnp.bfloat16)


def expert_kernel(*refs):
    near_left, near_right, far_left, far_right, near_packed, far_packed = refs[:6]
    row_weight, weight_in, weight_out, whole, near_out, far_out = refs[6:]
    near = jnp.concatenate([near_left[...], near_right[...]], axis=1)
    far = jnp.concatenate([far_left[...], far_right[...]], axis=1)
    packed = jnp.concatenate(
        [near_packed[...].astype(jnp.float32), far_packed[...].astype(jnp.float32)], axis=0
    ).astype(jnp.bfloat16)
    rows = jnp.concatenate([near, far, packed], axis=0)
    hidden_units, width = weight_out.shape
    tile = 256
    activated = []
    for start in range(0, hidden_units, tile):
        gate = jnp.dot(
            rows, weight_in[:, start : start + tile], preferred_element_type=jnp.float32
        )
        start += hidden_units
        up = jnp.dot(rows, weight_in[:, start : start + tile], preferred_element_type=jnp.float32)
        scaled = gate / (1.0 + jnp.exp(-gate)) * up * row_weight[...]
        activated.append(scaled.astype(jnp.bfloat16))
    activated = jnp.concatenate(activated, axis=1)
    count, capacity = whole.shape[0], near_out.shape[0]
    for start in range(0, width, tile):
        columns = slice(start, start + tile)
        reply = jnp.dot(activated, weight_out[:, columns], preferred_element_type=jnp.float32)
        whole[:, columns] = reply[:count]
        near_out[:, columns] = reply[count : count + capacity].astype(jnp.bfloat16)
        far_out[:, columns] = reply[count + capacity :].astype(jnp.bfloat16)


def unpack_kernel(index, far, pack, whole, returned, *outs):
    rows = pack.shape[2]
    total = lax.dot_general(
        pack[index],
        returned[...],
        (((0,), (0,)), ((), ())),
        preferred_element_type=jnp.float32,
    )
    total = total + whole[rows * far : rows * (far + 1), :]
    middle = outs[0].shape[1]
    for i, out in enumerate(outs):
        out[...] = total[:, i * middle : (i + 1) * middle].astype(out.dtype)


def final_kernel(state, *refs):
    parts, out = refs[:-1], refs[-1]
    middle = parts[0].shape[1]
    for i in range(2):
        columns = slice(i * middle, (i + 1) * middle)
        total = parts[i][...].astype(jnp.float32)
        for part in parts[2 + i :: 2]:
            total = total + part[...].astype(jnp.float32)
        out[:, columns] = (state[:, columns].astype(jnp.float32) + total).astype(jnp.bfloat16)


STEPS = (
    ("block", 4, 0),
    ("block", 8, 0),
    ("block", 2, 0),
    ("pack", 0),
    ("block", 2, 1),
    ("pack", 2),
    ("block", 4, 1),
    ("pack", 4),
    ("block", 8, 1),
    ("pack", 8),
    ("packed", 0),
    ("packed", 2),
    ("block", 6, 0),
    ("block", 12, 0),
    ("block", 10, 0),
    ("block", 6, 1),
    ("block", 12, 1),
    ("pack", 12),
    ("block", 14, 0),
    ("block", 10, 1),
    ("pack", 10),
    ("packed", 4),
    ("packed", 8),
    ("block", 14, 1),
    ("pack", 14),
    ("pack", 6),
    ("packed", 12),
    ("packed", 10),
    ("reply", 0),
    ("packed", 14),
    ("reply", 12),
    ("packed", 6),
)


def plain_steps(count):
    steps = [("pack", 0)]
    for mask in sorted(range(2, count, 2), key=lambda m: (m.bit_count(), m & 2, m)):
        steps += [("block", mask, 0), ("block", mask, 1), ("pack", mask)]
    return steps


def experts_sum(state, halves, pack, row_weight, weight_in, weight_out):
    ep_count = lax.axis_size("ep")
    rows, width = state.shape
    capacity = pack.shape[1]
    half = (rows, width // 2)
    packed_shape = jax.ShapeDtypeStruct((capacity, width), jnp.bfloat16)
    blocks, arrived = {0: halves}, {}
    replies, returned = {}, {}
    token = state

    def receive(mask, side):
        nonlocal token
        bit = mask & -mask
        source = blocks[mask ^ bit][side]
        if mask == 2:
            source = after(source, pack)
        token = after(swapped(source, "ep", bit), token)
        blocks.setdefault(mask, [None, None])[side] = token

    def send_packed(mask):
        nonlocal token
        token = local(
            functools.partial(pack_kernel, mask // 2),
            packed_shape,
            pack,
            blocks[mask][0],
            after(blocks[mask][1], token),
        )
        arrived[mask] = swapped(token, "ep", 1)

    def reply_to(mask):
        nonlocal token
        whole = jax.ShapeDtypeStruct((2 * rows, width), jnp.float32)
        replies[mask] = local(
            expert_kernel,
            [whole, packed_shape, packed_shape],
            after(blocks[mask][0], token),
            blocks[mask][1],
            *blocks[mask | 2],
            arrived[mask],
            arrived[mask | 2],
            row_weight[mask // 4],
            weight_in,
            weight_out,
            room=LARGE,
        )
        token = replies[mask][1]

    steps = STEPS if ep_count == 16 else plain_steps(ep_count)
    for kind, mask, *side in steps:
        if kind == "block":
            receive(mask, *side)
        elif kind == "pack":
            send_packed(mask)
        elif kind == "reply":
            reply_to(mask)
        else:
            token = arrived[mask] = after(arrived[mask], token)
    far = sorted(mask for mask in blocks if mask and not mask & 2)
    backward = [far[-1], far[-2]] + far[:-2][::-1] + [0]
    received = {mask: ([], []) for mask in backward}
    sums = {}

    def send_reply(mask):
        nonlocal token
        group, far_side = mask & ~2, mask // 2 % 2
        if group not in replies:
            reply_to(group)
        token = after(replies[group][1 + far_side], token)
        returned[mask] = swapped(token, "ep", 1)

    def unpack(mask):
        nonlocal token
        far_side = mask // 2 % 2
        kind = jnp.bfloat16 if far_side else jnp.float32
        outs = local(
            functools.partial(unpack_kernel, mask // 2, far_side),
            [jax.ShapeDtypeStruct(half, kind)] * 2,
            pack,
            replies[mask & ~2][0],
            after(returned[mask], token),
        )
        token = outs[0]
        if far_side:
            for side, out in enumerate(outs):
                received[mask & ~2][side].append(swapped(out, "ep", 2))
        else:
            sums[mask] = outs

    def pass_on(mask, side):
        nonlocal token
        total = sums[mask][side]
        for part in received[mask][side]:
            total = total + after(part, token).astype(jnp.float32)
        token = total.astype(jnp.bfloat16)
        bit = mask & -mask
        received[mask ^ bit][side].append(swapped(token, "ep", bit))

    for mask in backward[:2]:
        send_reply(mask | 2)
        send_reply(mask)
    unpack(backward[0] | 2)
    for mask in backward[2:-1]:
        send_reply(mask | 2)
        send_reply(mask)
    unpack(backward[0])
    for k, mask in enumerate(backward[1:-1]):
        if k == 0:
            unpack(mask | 2)
        pass_on(backward[k], 0)
        if k == 1:
            send_reply(2)
        pass_on(backward[k], 1)
        if k == 0:
            unpack(mask)
            unpack(backward[2] | 2)
        else:
            if k > 1:
                unpack(mask | 2)
            unpack(mask)
    send_reply(0)
    pass_on(backward[-2], 0)
    pass_on(backward[-2], 1)
    near, far = received[0]
    token = near[0] = after(near[0], token)
    unpack(2)
    token = far[0] = after(far[0], token)
    token = near[1] = after(near[1], token)
    unpack(0)
    parts = [part for pair in zip(*received[0]) for part in pair]
    shape = jax.ShapeDtypeStruct(state.shape, jnp.bfloat16)
    return local(final_kernel, shape, state, *sums[0], *parts)


def shards(
    queries,
    keys,
    values,
    prior_out,
    prior_lse,
    residual,
    out_proj,
    norm_gain,
    expert_in,
    expert_out,
    expert_ids,
    route_weight,
):
    local_rows = queries.shape[0]
    experts_all = lax.axis_size("ep") * expert_in.shape[0]
    top_count = expert_ids.shape[1]
    capacity = max(
        local_rows // 4, top_count * ((local_rows + experts_all - 2) // (experts_all - 1))
    )
    ep_count = lax.axis_size("ep")
    split = (
        lax.axis_size("ctx") == 2
        and out_proj.shape[0] * ep_count == HEADS // 2 * HD
        and 2 * out_proj.shape[0] == HD
    )
    picks = own_picks(expert_ids, route_weight)
    masks = [0]
    results = attention(queries, keys, values, prior_out, prior_lse, split)
    attended = results[0]
    if split:
        rows = out_proj.shape[0]
        given, kept = results[1:]
        sibling = swapped(given, "ctx", 1)
        planes, picks, masks = weight_planes(out_proj, picks, masks, given)
        given_sum, own_sum = product([sibling, kept], planes, rows)
        heard_sum = swapped(given_sum, "ctx", 1)
        picks = jnp.concatenate([picks] + [swapped(picks, "ep", m) for m in (1, 2, 3)], axis=0)
        masks = [mask | m for m in range(4) for mask in masks]
    else:
        picks, masks = all_picks(picks, masks, [1 << k for k in range(ep_count.bit_length() - 1)])
        full = lax.all_gather(out_proj, ("ctx", "ep"), axis=0, tiled=True)
        own_sum = jnp.dot(attended, full, preferred_element_type=jnp.float32)
        heard_sum = jnp.zeros_like(own_sum)
    pack, row_weight = routing(picks, masks, capacity)
    state, left, right = norm(own_sum, heard_sum, residual, norm_gain)
    layer_out = experts_sum(
        state, [left, right], pack, row_weight, expert_in[0], expert_out[0]
    )
    return (layer_out, attended)


def solution(mesh):
    return jax.shard_map(
        shards,
        mesh=mesh,
        in_specs=(
            P(("ctx", "ep"), None),
            P(("ctx", "ep"), None),
            P(("ctx", "ep"), None),
            P(("ctx", "ep"), None),
            P(("ctx", "ep"), None),
            P(("ctx", "ep"), None),
            P(("ctx", "ep"), None),
            P(),
            P("ep", None, None),
            P("ep", None, None),
            P(("ctx", "ep"), None),
            P(("ctx", "ep"), None),
        ),
        out_specs=(P(("ctx", "ep"), None), P(("ctx", "ep"), None)),
        check_vma=False,
    )
```
